256 devices in a mesh: wide: 32 (over x, z), narrow: 8 (over y, core).
Axes of the slice: x: 4, y: 4, z: 8, core: 2. Of those that a mesh axis runs over, the one named last changes fastest.
Arguments:
- ensemble: bfloat16 [1024, 262144], P('narrow', 'wide'), may hold values from -6 to 6
- owner: int32 [2048], P('wide'), may hold values from 0 to 255, as said below
- inflation: float32 [256], replicated, may hold values from 1 to 2
- obs_block: int32 [512], P('wide'), may hold values from 0 to 63
- obs_value: float32 [65536], P('wide'), may hold values from -12 to 12
- obs_std: float32 [65536], P('wide'), may hold values from 1 to 300
Outputs:
- analysis: bfloat16 [1024, 262144], P('narrow', 'wide')
The draws below stay inside these ranges and needn't reach their ends.
Inputs may be any that keep to these rules, and one draw needn't show every extreme that they name: `obs_block`: indexes one of the 64 state blocks held by the same index of wide as the observations. `owner`: a state block held by index w of wide belongs to one of the compartments w * 8 to w * 8 + 7.
All inputs are finite; a program needn't handle non-finite values.
Results may differ from the reference program's by a relative error of at most 0.0069.
Values may be sent and summed in bfloat16 or wider, within the bound.
A program may use at most 64 MiB of HBM per device.

```python
import math
import jax
import jax.numpy as jnp
from jax import lax

M = 1024
CLASSES = 128
S_DEV = 8192
P_DEV = 2048
COMP_DEV = 8
ITERS = 4
S = 262144
P_SIZE = 65536
NBLK_ALL = 2048
NOB = 512
COMP = 256
N_WIDE = 32


def draw_owner(key, part):
    key = jax.random.fold_in(key, 11)
    block_count = S_DEV // CLASSES
    positions = jnp.arange(NBLK_ALL, dtype=jnp.int32)
    base_comp = positions // block_count * COMP_DEV
    offsets = jax.random.randint(key, (NBLK_ALL,), 0, COMP_DEV, dtype=jnp.int32)
    offsets = jnp.where(positions == 0, 0, offsets)
    offsets = jnp.where(positions == NBLK_ALL - 1, COMP_DEV - 1, offsets)
    return (base_comp + offsets).astype(jnp.int32)


def plant(result, rng, low, largest):
    longest = result.shape.index(max(result.shape))
    spots = []
    for shift in (0, 1):
        where = [jax.random.randint(jax.random.fold_in(rng, axis), (), 0, length) for axis, length in enumerate(result.shape)]
        where[longest] = (where[longest] + shift) % result.shape[longest]
        spots.append(tuple(where))
    return result.at[spots[0]].set(low).at[spots[1]].set(largest)


def shard_levels(key, shape, cuts, smallest, top_value):
    def one(dim, parts):
        draws = jax.random.uniform(jax.random.fold_in(jax.random.fold_in(key, 6), dim), (parts,), jnp.float32, smallest / len(cuts), top_value / len(cuts))
        return jnp.repeat(jnp.exp(draws), shape[dim] // parts).reshape((-1,) + (1,) * (len(shape) - dim - 1))

    level = one(*cuts[0])
    for cut in cuts[1:]:
        level = level * one(*cut)
    return level


def centred(key, dims, deviation, reach, shards=(), held_as=jnp.bfloat16):
    array = jax.random.normal(key, dims, jnp.float32) * deviation
    if len(shards) > 0:
        array = shard_levels(key, dims, shards, -0.22, 0.18) * array
    return jnp.clip(array, min=-reach, max=reach).astype(held_as)


def setup_inputs(seed: int = 0) -> dict:
    key_list = jax.random.split(jax.random.key(seed), 7)
    ensemble = centred(key_list[0], (M, S), 1.0, 6.0, ((0, 8), (1, 32)))
    owner = draw_owner(jax.random.fold_in(key_list[6], 71), 0)
    inflation = jnp.clip(jax.random.uniform(key_list[2], (COMP,), jnp.float32, 1.0, 2.0), 1.0, 2.0)
    obs_block = plant(jax.random.randint(key_list[3], (NOB,), 0, S_DEV // CLASSES), jax.random.fold_in(key_list[3], 1), 0, (S_DEV // CLASSES) - 1).astype(jnp.int32)
    obs_value = centred(key_list[4], (P_SIZE,), 3.0, 12.0, ((0, 32),), jnp.float32)
    obs_std = jnp.clip(jnp.exp(math.log(300.0) - 5.7037825 * jax.random.uniform(key_list[5], (P_SIZE,), jnp.float32) ** shard_levels(key_list[5], (P_SIZE,), ((0, 32),), -0.2, 0.2)), 1.0, 300.0)
    return dict(ensemble=ensemble, owner=owner, inflation=inflation, obs_block=obs_block, obs_value=obs_value, obs_std=obs_std)


HIGH = lax.Precision.HIGHEST

def reference(ensemble, owner, inflation, obs_block, obs_value, obs_std):
    block_count = S_DEV // CLASSES
    obs_blocks = P_DEV // CLASSES
    scale_root = math.sqrt(M - 1)
    member_blocks = ensemble.reshape(M, N_WIDE, S_DEV).transpose(1, 0, 2)
    owner_ids = owner.reshape(N_WIDE, block_count)
    pick_rows = obs_block.reshape(N_WIDE, obs_blocks)
    obs_level = obs_value.reshape(N_WIDE, P_DEV)
    obs_sigma = obs_std.reshape(N_WIDE, P_DEV)

    def prepare(pieces):
        member_block, owner_part, pick_part, level_part, sigma_part = pieces
        state_mean = lax.optimization_barrier(jnp.sum(member_block, axis=0, dtype=jnp.float32)) / M
        row_factor = jnp.repeat(inflation[owner_part], CLASSES)
        anomaly = (row_factor * (member_block.astype(jnp.float32) - state_mean)).astype(jnp.bfloat16)
        observed = anomaly.reshape(M, block_count, CLASSES)[:, pick_part, :].reshape(M, P_DEV)
        observed_mean = state_mean.reshape(block_count, CLASSES)[pick_part].reshape(P_DEV)
        scaled = (observed.astype(jnp.float32) / (sigma_part * scale_root)).astype(jnp.bfloat16)
        innovation = (level_part - observed_mean) / sigma_part
        gram_part = jnp.dot(scaled, scaled.T, preferred_element_type=jnp.float32)
        projected_part = jnp.dot(scaled.astype(jnp.float32), innovation, precision=HIGH)
        return (state_mean, anomaly, gram_part, projected_part)
    means, anomalies, gram_parts, projected_parts = lax.map(prepare, (member_blocks, owner_ids, pick_rows, obs_level, obs_sigma))
    identity = jnp.eye(M, dtype=jnp.float32)
    gram_matrix = lax.optimization_barrier(jnp.sum(gram_parts, axis=0)) + identity
    projected = lax.optimization_barrier(jnp.sum(projected_parts, axis=0))
    frob_norm = jnp.sqrt(jnp.sum(gram_matrix * gram_matrix))
    unit_gram = gram_matrix / frob_norm
    iterate = identity
    for turn_index in range(ITERS):
        product_one = jnp.dot(unit_gram, iterate, precision=HIGH)
        product_two = jnp.dot(product_one, iterate, precision=HIGH)
        iterate = 1.5 * iterate - 0.5 * jnp.dot(product_two, iterate, precision=HIGH)
    root_matrix = iterate / jnp.sqrt(frob_norm)
    midway = jnp.dot(root_matrix, projected, precision=HIGH)
    mean_shift = jnp.dot(root_matrix, midway, precision=HIGH) / scale_root
    transform = (root_matrix + mean_shift[:, None]).astype(jnp.bfloat16)

    def apply_transform(pieces):
        state_mean, anomaly = pieces
        update = jnp.dot(transform.T, anomaly, preferred_element_type=jnp.float32)
        return (state_mean[None, :] + update).astype(jnp.bfloat16)
    outputs = lax.map(apply_transform, (means, anomalies))
    return outputs.transpose(1, 0, 2).reshape(M, S)
```

```python
import functools
import math

import jax
import jax.numpy as jnp
from jax import lax
from jax.experimental import pallas as pl
from jax.experimental.pallas import tpu as pltpu
from jax.sharding import PartitionSpec as P

CLASSES = 128
ITERS = 4
MESH = pl.DeviceIdType.MESH
F32 = jnp.float32
BF16 = jnp.bfloat16
NT = (((1,), (1,)), ((), ()))


class Plan:
    def __init__(self, grid, narrow, local_members, local_states, obs_local):
        self.nx, self.nz = grid
        self.narrow = narrow
        self.ny = narrow // 2
        self.ml = local_members
        self.m = local_members * narrow
        self.states = local_states
        self.share = local_states // narrow
        self.obs = obs_local
        self.oshare = obs_local // narrow
        self.nb = self.m // 128
        self.blocks = [(i, j) for i in range(self.nb) for j in range(i, self.nb)]
        self.half = len(self.blocks) // 2
        self.peers = self.nx * self.ny
        self.rows = self.half * 128 // self.peers
        self.tall = self.rows + 16
        self.strip = min(256, self.m)
        assert self.half * 2 == len(self.blocks) and self.rows % 16 == 0
        assert local_members == 128 and self.rows * self.peers == self.half * 128


def segments(plan, pos):
    out, row = [], pos * 128
    while row < (pos + 1) * 128:
        piece, inside = divmod(row, plan.rows)
        count = min(plan.rows - inside, (pos + 1) * 128 - row)
        out.append((piece, inside, row - pos * 128, count))
        row += count
    return out


def resplit(tail, nb):
    total = tail[:nb] + tail[nb : 2 * nb]
    high = total.astype(BF16).astype(F32)
    rest = [high, total - high]
    if 2 * nb < 16:
        rest.append(jnp.zeros((16 - 2 * nb, 128), F32))
    return jnp.concatenate(rest, axis=0)


def kernel(plan, owner, infl, oblk, ens, value, std, out, ens_v, gat, robs, scaled, part, corebuf, chipsum, xybuf,
           zbuf, tailbuf, prow, agbuf, gram, prod, mix, est, estb, raw, anom, tmat, stage, load_sem, obs_s, obs_r,
           core_s, core_r, xy_s, xy_r, z_s, z_r, ag_s, ag_r, fw_s, fw_r, raw_s, raw_r, own_sem, out_s, out_r):
    p = plan
    n = lax.axis_index("narrow")
    w = lax.axis_index("wide")
    x, z = lax.div(w, p.nz), lax.rem(w, p.nz)
    y, c = lax.div(n, 2), lax.rem(n, 2)
    q0 = x * p.ny + y
    root_scale = math.sqrt(p.m - 1)

    def copy_to(src, dst, send, recv, device):
        return pltpu.make_async_remote_copy(
            src_ref=src, dst_ref=dst, send_sem=send, recv_sem=recv, device_id=device, device_id_type=MESH
        )

    def near(t):
        return lax.rem(n + t, p.narrow)

    def along(t):
        return lax.rem(z + t, p.nz)

    def plane(t):
        return lax.rem(q0 + t, p.peers)

    def plane_id(q):
        return (lax.div(q, p.ny) * p.nz + z, lax.rem(q, p.ny) * 2 + c)

    sibling = (w, n + 1 - 2 * c)

    def load_block(b):
        cols = pl.ds(pl.multiple_of(b * 128, 128), 128)
        return pltpu.make_async_copy(ens.at[:, cols], ens_v.at[b], load_sem)

    count = p.states // 128
    lax.fori_loop(0, count, lambda b, carry: (load_block(b).start(), carry)[1], 0)

    barrier = pltpu.get_barrier_semaphore()
    greeted = 0
    for t in range(1, p.narrow):
        pl.semaphore_signal(barrier, inc=1, device_id=(w, near(t)), device_id_type=MESH)
        greeted += 1
    for t in range(1, p.nz):
        pl.semaphore_signal(barrier, inc=1, device_id=(x * p.nz + along(t), n), device_id_type=MESH)
        greeted += 1
    for dx in range(1, p.nx):
        for dy in range(p.ny):
            there = (lax.rem(x + dx, p.nx) * p.nz + z, lax.rem(y + dy, p.ny) * 2 + c)
            pl.semaphore_signal(barrier, inc=1, device_id=there, device_id_type=MESH)
            greeted += 1

    pltpu.make_async_copy(ens_v, ens_v, load_sem).wait()
    per = p.oshare // 128
    for b in range(p.obs // 128):
        gat[b // per, :, (b % per) * 128 : (b % per) * 128 + 128] = ens_v[oblk[b]]
    pl.semaphore_wait(barrier, greeted)

    def obs_copy(t):
        there = near(t)
        return copy_to(gat.at[there], robs.at[n], obs_s.at[t], obs_r.at[n], (w, there))

    def obs_arrival(t):
        frm = near(t)
        return copy_to(gat.at[frm], robs.at[frm], obs_s.at[t], obs_r.at[frm], (w, frm))

    for t in range(1, p.narrow):
        obs_copy(t).start()
    robs[pl.ds(n, 1)] = gat[pl.ds(n, 1)]
    for t in range(1, p.narrow):
        obs_arrival(t).wait_recv()

    innov = []
    for k in range(per):
        cols = slice(k * 128, k * 128 + 128)
        member = robs[:, :, cols].reshape(p.m, 128).astype(F32)
        mean = jnp.sum(member, axis=0, keepdims=True) / p.m
        ob = n * per + k
        factor = infl[owner[oblk[ob]]]
        sigma = std[pl.ds(ob, 1), :]
        shifted = (factor * (member - mean)).astype(BF16)
        scaled[:, cols] = (shifted.astype(F32) / (sigma * root_scale)).astype(BF16)
        innov.append((value[pl.ds(ob, 1), :] - mean) / sigma)
    innov = jnp.concatenate(innov, axis=1)
    high = innov.astype(BF16).astype(F32)
    middle = (innov - high).astype(BF16).astype(F32)
    low = innov - high - middle
    row_ids = lax.broadcasted_iota(jnp.int32, (16, p.oshare), 0)
    lhs = jnp.where(row_ids == 0, high, jnp.where(row_ids == 1, middle, jnp.where(row_ids == 2, low, 0.0)))
    projected = lax.dot_general(lhs.astype(BF16), scaled[...], NT, preferred_element_type=F32)
    projected = jnp.sum(projected, axis=0, keepdims=True)
    tailbuf[...] = jnp.zeros_like(tailbuf)
    for i in range(p.nb):
        tailbuf[i : i + 1, :] = projected[:, i * 128 : i * 128 + 128]
    tail = resplit(tailbuf[...], p.nb).astype(BF16)
    for h in range(2):
        for piece in range(p.peers):
            part[h, piece, p.rows : p.tall, :] = tail
    index = 0
    for i in range(p.nb):
        rows = lax.dot_general(
            scaled[i * 128 : i * 128 + 128, :], scaled[i * 128 :, :], NT, preferred_element_type=F32
        ).astype(BF16)
        for j in range(i, p.nb):
            h, pos = divmod(index, p.half)
            for piece, inside, start, count in segments(p, pos):
                part[h, piece, inside : inside + count, :] = rows[start : start + count, (j - i) * 128 : (j - i) * 128 + 128]
            index += 1

    core_copy = copy_to(part.at[1 - c], corebuf, core_s, core_r, sibling)
    core_copy.start()
    core_copy.wait_recv()
    tail = part[c, 0, p.rows : p.tall, :].astype(F32) + corebuf[0, p.rows : p.tall, :].astype(F32)
    tail = resplit(tail, p.nb).astype(BF16)

    def chip_add(piece, carry):
        total = part[c, piece, : p.rows, :].astype(F32) + corebuf[piece, : p.rows, :].astype(F32)
        chipsum[piece, : p.rows, :] = total.astype(BF16)
        chipsum[piece, p.rows : p.tall, :] = tail
        return carry

    lax.fori_loop(0, p.peers, chip_add, 0)

    def xy_copy(t):
        there = plane(t)
        return copy_to(chipsum.at[there], xybuf.at[q0], xy_s.at[t], xy_r.at[q0], plane_id(there))

    def xy_arrival(t):
        frm = plane(t)
        return copy_to(chipsum.at[frm], xybuf.at[frm], xy_s.at[t], xy_r.at[frm], plane_id(frm))

    lax.fori_loop(1, p.peers, lambda t, carry: (xy_copy(t).start(), carry)[1], 0)

    def xy_add(t, total):
        xy_arrival(t).wait_recv()
        return total + xybuf[plane(t)].astype(F32)

    total = lax.fori_loop(1, p.peers, xy_add, chipsum[q0].astype(F32))
    zbuf[z, : p.rows, :] = total[: p.rows].astype(BF16)
    zbuf[z, p.rows : p.tall, :] = resplit(total[p.rows :], p.nb).astype(BF16)

    def z_copy(t):
        there = along(t)
        return copy_to(zbuf.at[z], zbuf.at[z], z_s.at[t], z_r.at[z], (x * p.nz + there, n))

    def z_arrival(t):
        frm = along(t)
        return copy_to(zbuf.at[frm], zbuf.at[frm], z_s.at[t], z_r.at[frm], (x * p.nz + frm, n))

    for t in range(1, p.nz):
        z_copy(t).start()
    for t in range(1, p.nz):
        z_arrival(t).wait_recv()
    total = zbuf[0].astype(F32)
    for k in range(1, p.nz):
        total = total + zbuf[k].astype(F32)

    def piece_rows(q):
        return pl.ds(pl.multiple_of(q * p.rows, 16), p.rows)

    agbuf[c, piece_rows(q0), :] = total[: p.rows].astype(BF16)
    for i in range(p.nb):
        prow[:, i * 128 : i * 128 + 128] = total[p.rows + i : p.rows + i + 1] + total[p.rows + p.nb + i : p.rows + p.nb + i + 1]

    def ag_copy(t):
        mine = agbuf.at[c, piece_rows(q0), :]
        return copy_to(mine, mine, ag_s.at[t], ag_r.at[q0], plane_id(plane(t)))

    def ag_arrival(t):
        frm = plane(t)
        slot = agbuf.at[c, piece_rows(frm), :]
        return copy_to(slot, slot, ag_s.at[t], ag_r.at[frm], plane_id(frm))

    def forward(q):
        slot = agbuf.at[c, piece_rows(q), :]
        return copy_to(slot, slot, fw_s.at[q], fw_r.at[q], sibling)

    def forward_arrival(q):
        slot = agbuf.at[1 - c, piece_rows(q), :]
        return copy_to(slot, slot, fw_s.at[q], fw_r.at[q], sibling)

    lax.fori_loop(1, p.peers, lambda t, carry: (ag_copy(t).start(), carry)[1], 0)
    forward(q0).start()

    def pass_on(t, carry):
        ag_arrival(t).wait_recv()
        forward(plane(t)).start()
        return carry

    lax.fori_loop(1, p.peers, pass_on, 0)

    def share_cols(k):
        return pl.ds(pl.multiple_of(k * p.share, 128), p.share)

    def raw_copy(t):
        there = near(t)
        return copy_to(ens.at[:, share_cols(there)], raw.at[n], raw_s.at[t], raw_r.at[n], (w, there))

    def raw_arrival(t):
        frm = near(t)
        return copy_to(ens.at[:, share_cols(frm)], raw.at[frm], raw_s.at[t], raw_r.at[frm], (w, frm))

    for t in range(1, p.narrow):
        raw_copy(t).start()
    own = pltpu.make_async_copy(ens.at[:, share_cols(n)], raw.at[n], own_sem)
    own.start()
    lax.fori_loop(0, p.peers, lambda q, carry: (forward_arrival(q).wait_recv(), carry)[1], 0)

    diag = lax.broadcasted_iota(jnp.int32, (128, 128), 0) == lax.broadcasted_iota(jnp.int32, (128, 128), 1)
    eye = diag.astype(F32)
    square = jnp.zeros((128, 128), F32)
    index = 0
    for i in range(p.nb):
        for j in range(i, p.nb):
            h, pos = divmod(index, p.half)
            block = agbuf[h, pos * 128 : pos * 128 + 128, :]
            wide = block.astype(F32)
            if i == j:
                wide = wide + eye
                block = wide.astype(BF16)
                square = square + wide * wide
            else:
                square = square + 2.0 * (wide * wide)
                gram[j * 128 : j * 128 + 128, i * 128 : i * 128 + 128] = wide.T.astype(BF16)
            gram[i * 128 : i * 128 + 128, j * 128 : j * 128 + 128] = block
            index += 1
    square = jnp.sum(jnp.sum(square, axis=0, keepdims=True), axis=1, keepdims=True)
    frob = jnp.sqrt(square)
    inv = 1.0 / frob

    strips = p.m // p.strip

    def cols_of(s):
        return pl.ds(pl.multiple_of(s * p.strip, 128), p.strip)

    def mm(a, b):
        return jnp.dot(a, b, preferred_element_type=F32)

    def first(s, carry):
        cols = cols_of(s)
        unit = gram[:, cols].astype(F32) * inv
        unit2 = mm(gram[...], gram[:, cols]) * (inv * inv)
        prod[:, cols] = unit2.astype(BF16)
        mix[:, cols] = (0.0625 * unit2 - 0.5625 * unit).astype(BF16)
        est[:, cols] = 1.6875 * unit2 - 2.4375 * unit
        return carry

    def second(s, carry):
        cols = cols_of(s)
        new = est[:, cols] + mm(prod[...], mix[:, cols])
        est[:, cols] = new
        estb[:, cols] = new.astype(BF16)
        return carry

    lax.fori_loop(0, strips, first, 0)
    lax.fori_loop(0, strips, second, 0)
    level = 2.25
    for turn in range(2, ITERS):
        last = turn == ITERS - 1

        def left(s, carry, level=level):
            cols = cols_of(s)
            old = est[:, cols]
            unit_it = gram[:, cols].astype(F32) * (level * inv) + mm(gram[...], estb[:, cols]) * inv
            prod[:, cols] = unit_it.astype(BF16)
            mix[:, cols] = (2.0 * level * old + mm(estb[...], estb[:, cols])).astype(BF16)
            est[:, cols] = 1.5 * old - (0.5 * level * level) * unit_it
            return carry

        def right(s, carry, level=level, last=last):
            cols = cols_of(s)
            new = est[:, cols] - 0.5 * mm(prod[...], mix[:, cols])
            if last:
                row_ids = lax.broadcasted_iota(jnp.int32, (p.m, p.strip), 0)
                col_ids = lax.broadcasted_iota(jnp.int32, (p.m, p.strip), 1) + s * p.strip
                est[:, cols] = new + jnp.where(row_ids == col_ids, 1.5 * level, 0.0)
            else:
                est[:, cols] = new
                estb[:, cols] = new.astype(BF16)
            return carry

        lax.fori_loop(0, strips, left, 0)
        lax.fori_loop(0, strips, right, 0)
        level = 1.5 * level

    inv_root = lax.rsqrt(frob)

    def shift_rows(s, total):
        rows = pl.ds(pl.multiple_of(s * 128, 128), 128)
        block = est[rows, :]
        midway = jnp.sum(block * prow[...], axis=1, keepdims=True)
        return total + jnp.sum(block * midway, axis=0, keepdims=True)

    shift = lax.fori_loop(0, p.m // 128, shift_rows, jnp.zeros((1, p.m), F32))
    shift = shift * (inv / root_scale)

    def transform_rows(s, carry):
        rows = pl.ds(pl.multiple_of(s * 128, 128), 128)
        tmat[rows, :] = (est[rows, :] * inv_root + shift).astype(BF16)
        return carry

    lax.fori_loop(0, p.m // 128, transform_rows, 0)

    for t in range(1, p.narrow):
        raw_arrival(t).wait_recv()
    own.wait()
    state_mean = jnp.zeros((1, p.share), F32)
    for k in range(p.narrow):
        state_mean = state_mean + jnp.sum(raw[k].astype(F32), axis=0, keepdims=True)
    state_mean = state_mean / p.m
    factors = [
        jnp.full((1, 128), infl[owner[n * (p.share // 128) + b]], F32) for b in range(p.share // 128)
    ]
    factors = jnp.concatenate(factors, axis=1)
    for k in range(p.narrow):
        anom[k * 128 : k * 128 + 128, :] = (factors * (raw[k].astype(F32) - state_mean)).astype(BF16)

    def out_copy(dy, core):
        there = lax.rem(y + dy, p.ny) * 2 + core
        return copy_to(
            stage.at[dy, pl.ds(core * 128, 128), :], out.at[:, share_cols(n)], out_s.at[dy, core],
            out_r.at[n], (w, there)
        )

    def out_arrival(frm):
        return copy_to(
            stage.at[0, pl.ds(0, 128), :], out.at[:, share_cols(frm)], out_s.at[0, 0], out_r.at[frm], (w, frm)
        )

    def analyse(dy):
        rows = pl.ds(pl.multiple_of(lax.rem(y + dy, p.ny) * 256, 256), 256)
        stage[dy] = (state_mean + mm(tmat[rows, :], anom[...])).astype(BF16)

    order = sorted(range(1, p.ny), key=lambda d: -min(d, p.ny - d))
    for dy in order:
        analyse(dy)
        for core in range(2):
            out_copy(dy, core).start()
    analyse(0)
    to_sibling = copy_to(
        stage.at[0, pl.ds(pl.multiple_of((1 - c) * 128, 128), 128), :], out.at[:, share_cols(n)], out_s.at[0, 0], out_r.at[n], sibling
    )
    to_sibling.start()
    keep = pltpu.make_async_copy(
        stage.at[0, pl.ds(pl.multiple_of(c * 128, 128), 128), :], out.at[:, share_cols(n)], own_sem
    )
    keep.start()

    for t in range(1, p.narrow):
        out_arrival(near(t)).wait_recv()
    keep.wait()
    to_sibling.wait_send()
    for dy in order:
        for core in range(2):
            out_copy(dy, core).wait_send()
    for t in range(1, p.narrow):
        obs_copy(t).wait_send()
        raw_copy(t).wait_send()
    core_copy.wait_send()
    for t in range(1, p.nz):
        z_copy(t).wait_send()

    def drain(t, carry):
        xy_copy(t).wait_send()
        ag_copy(t).wait_send()
        return carry

    lax.fori_loop(1, p.peers, drain, 0)
    lax.fori_loop(0, p.peers, lambda q, carry: (forward(q).wait_send(), carry)[1], 0)


def on_device(grid, narrow, ensemble, owner, inflation, obs_block, obs_value, obs_std):
    p = Plan(grid, narrow, *ensemble.shape, obs_value.shape[0])
    dma = pltpu.SemaphoreType.DMA
    vmem, smem = pl.BlockSpec(memory_space=pltpu.VMEM), pl.BlockSpec(memory_space=pltpu.SMEM)
    anywhere = pl.BlockSpec(memory_space=pl.ANY)
    square = (p.m, p.m)
    scratch = [
        pltpu.VMEM((p.states // 128, p.ml, 128), BF16),
        pltpu.VMEM((p.narrow, p.ml, p.oshare), BF16),
        pltpu.VMEM((p.narrow, p.ml, p.oshare), BF16),
        pltpu.VMEM((p.m, p.oshare), BF16),
        pltpu.VMEM((2, p.peers, p.tall, 128), BF16),
        pltpu.VMEM((p.peers, p.tall, 128), BF16),
        pltpu.VMEM((p.peers, p.tall, 128), BF16),
        pltpu.VMEM((p.peers, p.tall, 128), BF16),
        pltpu.VMEM((p.nz, p.tall, 128), BF16),
        pltpu.VMEM((16, 128), F32),
        pltpu.VMEM((1, p.m), F32),
        pltpu.VMEM((2, p.peers * p.rows, 128), BF16),
        pltpu.VMEM(square, BF16),
        pltpu.VMEM(square, BF16),
        pltpu.VMEM(square, BF16),
        pltpu.VMEM(square, F32),
        pltpu.VMEM(square, BF16),
        pltpu.VMEM((p.narrow, p.ml, p.share), BF16),
        pltpu.VMEM((p.m, p.share), BF16),
        pltpu.VMEM(square, BF16),
        pltpu.VMEM((p.ny, 256, p.share), BF16),
        dma, dma((p.narrow,)), dma((p.narrow,)),
        dma, dma,
        dma((p.peers,)), dma((p.peers,)),
        dma((p.nz,)), dma((p.nz,)),
        dma((p.peers,)), dma((p.peers,)),
        dma((p.peers,)), dma((p.peers,)),
        dma((p.narrow,)), dma((p.narrow,)),
        dma, dma((p.ny, 2)), dma((p.narrow,)),
    ]
    return pl.pallas_call(
        functools.partial(kernel, p),
        out_shape=jax.ShapeDtypeStruct(ensemble.shape, BF16),
        in_specs=[smem, smem, smem, anywhere, vmem, vmem],
        out_specs=anywhere,
        scratch_shapes=scratch,
        compiler_params=pltpu.CompilerParams(
            collective_id=0, has_side_effects=True, vmem_limit_bytes=56 * 1024 * 1024
        ),
        name="etkf",
    )(owner, inflation, obs_block, ensemble, obs_value.reshape(-1, 128), obs_std.reshape(-1, 128))


def solution(mesh):
    wide, narrow = mesh.shape["wide"], mesh.shape["narrow"]
    grid = (4, wide // 4) if wide >= 16 else (2, wide // 2)
    return jax.shard_map(
        functools.partial(on_device, grid, narrow),
        mesh=mesh,
        in_specs=(P("narrow", "wide"), P("wide"), P(), P("wide"), P("wide"), P("wide")),
        out_specs=P("narrow", "wide"),
        check_vma=False,
    )
```

```python
import functools
import math

import jax
import jax.numpy as jnp
from jax import lax
from jax.experimental import pallas as pl
from jax.experimental.pallas import tpu as pltpu
from jax.sharding import PartitionSpec as P

CLASSES = 128
MESH = pl.DeviceIdType.MESH
F32 = jnp.float32
BF16 = jnp.bfloat16
NT = (((1,), (1,)), ((), ()))
RAW_AT = ((None, None, 0, 0), (4, 4, 4, 4), (0, 1, 2, 4))


class Plan:
    def __init__(self, grid, narrow, local_members, local_states, obs_local):
        self.nx, self.nz = grid
        self.narrow = narrow
        self.ny = narrow // 2
        self.ml = local_members
        self.m = local_members * narrow
        self.states = local_states
        self.share = local_states // narrow
        self.obs = obs_local
        self.oshare = obs_local // narrow
        self.nb = self.m // 128
        self.blocks = [(i, j) for i in range(self.nb) for j in range(i, self.nb)]
        self.half = len(self.blocks) // 2
        self.peers = self.nx * self.ny
        tiles = self.half * 8
        self.ra = tiles * 2 // 3 // self.peers * 16
        self.rb = (tiles * 16 - self.ra * self.peers) // self.nz
        self.tb = self.rb + 16
        self.base = self.ra * self.peers
        self.strip = min(256, self.m)
        assert self.half * 2 == len(self.blocks) and self.rb % 16 == 0
        assert local_members == 128 and self.base + self.rb * self.nz == self.half * 128
        self.near = sorted(((d, f) for d in range(self.ny) for f in range(2) if d + f), key=lambda k: -min(k[0], self.ny - k[0]))


def segments(plan, pos):
    out, row = [], pos * 128
    while row < (pos + 1) * 128:
        first = row < plan.base
        size = plan.ra if first else plan.rb
        piece, inside = divmod(row if first else row - plan.base, size)
        count = min(size - inside, (pos + 1) * 128 - row)
        out.append((first, piece, inside, row - pos * 128, count))
        row += count
    return out


def resplit(tail, nb):
    total = tail[:nb] + tail[nb : 2 * nb]
    high = total.astype(BF16).astype(F32)
    rest = [high, total - high]
    if 2 * nb < 16:
        rest.append(jnp.zeros((16 - 2 * nb, 128), F32))
    return jnp.concatenate(rest, axis=0)


def kernel(plan, owner, infl, oblk, ens, value, std, out, ens_v, gat, robs, scaled, part_a, part_b, core_a, core_b, chip_a,
           chip_b, xy_a, z_b, z_a, x_b, y_b, tailbuf, prow, agbuf, gram, prod, mix, est, estb, more, moreb, raw, anom, tmat, stage,
           load_sem, obs_s, obs_r, core_s, core_r, xa_s, xa_r, zb_s, zb_r, za_s, za_r, xb_s, xb_r, yb_s, yb_r, ga_s, ga_r, gb_s, gb_r,
           fa_s, fa_r, fb_s, fb_r, raw_s, raw_r, own_sem, out_s, out_r):
    p = plan
    n = lax.axis_index("narrow")
    w = lax.axis_index("wide")
    x, z = lax.div(w, p.nz), lax.rem(w, p.nz)
    y, c = lax.div(n, 2), lax.rem(n, 2)
    q0 = x * p.ny + y
    root_scale = math.sqrt(p.m - 1)
    pending = []

    def copy_to(src, dst, send, recv, device):
        return pltpu.make_async_remote_copy(
            src_ref=src, dst_ref=dst, send_sem=send, recv_sem=recv, device_id=device, device_id_type=MESH
        )

    def near(k):
        return lax.rem(y + k[0], p.ny) * 2 + (1 - c if k[1] else c)

    def along(t):
        return lax.rem(z + t, p.nz)

    def along_id(k):
        return (x * p.nz + k, n)

    def plane(t):
        return lax.rem(q0 + t, p.peers)

    def plane_id(q):
        return (lax.div(q, p.ny) * p.nz + z, lax.rem(q, p.ny) * 2 + c)

    sibling = (w, n + 1 - 2 * c)

    def each(count, step):
        def body(t, carry):
            step(t)
            return carry

        lax.fori_loop(1, count, body, 0)

    def finish(items):
        for item in items:
            if isinstance(item, tuple):
                each(item[0], lambda t: item[1](t).wait_send())
            else:
                item.wait_send()

    def load_block(b):
        cols = pl.ds(pl.multiple_of(b * 128, 128), 128)
        return pltpu.make_async_copy(ens.at[:, cols], ens_v.at[b], load_sem)

    count = p.states // 128
    lax.fori_loop(0, count, lambda b, carry: (load_block(b).start(), carry)[1], 0)

    barrier = pltpu.get_barrier_semaphore()
    greeted = 0
    for k in p.near:
        pl.semaphore_signal(barrier, inc=1, device_id=(w, near(k)), device_id_type=MESH)
        greeted += 1
    for t in range(1, p.nz):
        pl.semaphore_signal(barrier, inc=1, device_id=along_id(along(t)), device_id_type=MESH)
        greeted += 1
    for dx in range(1, p.nx):
        for dy in range(p.ny):
            there = (lax.rem(x + dx, p.nx) * p.nz + z, lax.rem(y + dy, p.ny) * 2 + c)
            pl.semaphore_signal(barrier, inc=1, device_id=there, device_id_type=MESH)
            greeted += 1

    pltpu.make_async_copy(ens_v, ens_v, load_sem).wait()
    per = p.oshare // 128
    for b in range(p.obs // 128):
        gat[b // per, :, (b % per) * 128 : (b % per) * 128 + 128] = ens_v[oblk[b]]
    pl.semaphore_wait(barrier, greeted)

    def obs_copy(k):
        there = near(k)
        return copy_to(gat.at[there], robs.at[n], obs_s.at[2 * k[0] + k[1]], obs_r.at[n], (w, there))

    def obs_arrival(k):
        frm = near(k)
        return copy_to(gat.at[frm], robs.at[frm], obs_s.at[0], obs_r.at[frm], (w, frm))

    for k in p.near:
        obs_copy(k).start()
        pending.append(obs_copy(k))
    robs[pl.ds(n, 1)] = gat[pl.ds(n, 1)]
    for k in p.near:
        obs_arrival(k).wait_recv()

    def share_cols(k):
        return pl.ds(pl.multiple_of(k * p.share, 128), p.share)

    def half_cols(k, h):
        return pl.ds(pl.multiple_of(k * p.share + h * (p.share // 2), 128), p.share // 2)

    def half_slot(k, h):
        return raw.at[k, :, pl.ds(h * (p.share // 2), p.share // 2)]

    def raw_copy(k, h):
        there = near(k)
        src = ens.at[:, half_cols(there, h)]
        return copy_to(src, half_slot(n, h), raw_s.at[2 * k[0] + k[1], h], raw_r.at[n, h], (w, there))

    def raw_arrival(k, h):
        frm = near(k)
        return copy_to(ens.at[:, half_cols(frm, h)], half_slot(frm, h), raw_s.at[0, 0], raw_r.at[frm, h], (w, frm))

    def raw_start(when):
        for k in p.near:
            for h in range(2):
                if RAW_AT[min(k[0], p.ny - k[0])][2 * k[1] + h] == when:
                    raw_copy(k, h).start()
                    pending.append(raw_copy(k, h))

    own = pltpu.make_async_copy(ens.at[:, share_cols(n)], raw.at[n], own_sem)
    own.start()
    raw_start(0)

    innov = []
    for k in range(per):
        cols = slice(k * 128, k * 128 + 128)
        member = robs[:, :, cols].reshape(p.m, 128).astype(F32)
        mean = jnp.sum(member, axis=0, keepdims=True) / p.m
        ob = n * per + k
        factor = infl[owner[oblk[ob]]]
        sigma = std[pl.ds(ob, 1), :]
        shifted = (factor * (member - mean)).astype(BF16)
        scaled[:, cols] = (shifted.astype(F32) / (sigma * root_scale)).astype(BF16)
        innov.append((value[pl.ds(ob, 1), :] - mean) / sigma)
    innov = jnp.concatenate(innov, axis=1)
    high = innov.astype(BF16).astype(F32)
    middle = (innov - high).astype(BF16).astype(F32)
    low = innov - high - middle
    row_ids = lax.broadcasted_iota(jnp.int32, (16, p.oshare), 0)
    lhs = jnp.where(row_ids == 0, high, jnp.where(row_ids == 1, middle, jnp.where(row_ids == 2, low, 0.0)))
    projected = lax.dot_general(lhs.astype(BF16), scaled[...], NT, preferred_element_type=F32)
    projected = jnp.sum(projected, axis=0, keepdims=True)
    tailbuf[...] = jnp.zeros_like(tailbuf)
    for i in range(p.nb):
        tailbuf[i : i + 1, :] = projected[:, i * 128 : i * 128 + 128]
    tail = resplit(tailbuf[...], p.nb).astype(BF16)
    for h in range(2):
        part_b[h, 0, p.rb :, :] = tail
        for k in range(1, p.nz):
            part_b[h, k, p.rb :, :] = jnp.zeros_like(tail)
    index = 0
    for i in range(p.nb):
        rows = lax.dot_general(
            scaled[i * 128 : i * 128 + 128, :], scaled[i * 128 :, :], NT, preferred_element_type=F32
        ).astype(BF16)
        for j in range(i, p.nb):
            h, pos = divmod(index, p.half)
            for first, piece, inside, start, count in segments(p, pos):
                ref = part_a if first else part_b
                ref[h, piece, inside : inside + count, :] = rows[start : start + count, (j - i) * 128 : (j - i) * 128 + 128]
            index += 1

    core_copy_b = copy_to(part_b.at[1 - c], core_b, core_s.at[0], core_r.at[0], sibling)
    core_copy_a = copy_to(part_a.at[1 - c], core_a, core_s.at[1], core_r.at[1], sibling)
    core_copy_b.start()
    core_copy_a.start()
    pending += [core_copy_a, core_copy_b]

    def zb_copy(t):
        there = along(t)
        return copy_to(chip_b.at[there], z_b.at[z], zb_s.at[t], zb_r.at[z], along_id(there))

    def zb_arrival(t):
        frm = along(t)
        return copy_to(chip_b.at[frm], z_b.at[frm], zb_s.at[0], zb_r.at[frm], along_id(frm))

    def xa_copy(t):
        there = plane(t)
        return copy_to(chip_a.at[there], xy_a.at[q0], xa_s.at[t], xa_r.at[q0], plane_id(there))

    def xa_arrival(t):
        frm = plane(t)
        return copy_to(chip_a.at[frm], xy_a.at[frm], xa_s.at[0], xa_r.at[frm], plane_id(frm))

    def add_b(k, carry):
        total = part_b[c, k, : p.rb, :].astype(F32) + core_b[k, : p.rb, :].astype(F32)
        chip_b[k, : p.rb, :] = total.astype(BF16)
        chip_b[k, p.rb :, :] = tail
        return carry

    def add_a(k, carry):
        chip_a[k] = (part_a[c, k].astype(F32) + core_a[k].astype(F32)).astype(BF16)
        return carry

    core_copy_b.wait_recv()
    tail = resplit(part_b[c, 0, p.rb :, :].astype(F32) + core_b[0, p.rb :, :].astype(F32), p.nb).astype(BF16)
    lax.fori_loop(0, p.nz, add_b, 0)
    each(p.nz, lambda t: zb_copy(t).start())
    core_copy_a.wait_recv()
    lax.fori_loop(0, p.peers, add_a, 0)
    each(p.peers, lambda t: xa_copy(t).start())
    pending += [(p.nz, zb_copy), (p.peers, xa_copy)]
    raw_start(1)

    def za_copy(t):
        return copy_to(z_a.at[z], z_a.at[z], za_s.at[t], za_r.at[z], along_id(along(t)))

    def za_arrival(t):
        frm = along(t)
        return copy_to(z_a.at[frm], z_a.at[frm], za_s.at[0], za_r.at[frm], along_id(frm))

    def x_id(t):
        return (lax.rem(x + t, p.nx) * p.nz + z, n)

    def y_id(t):
        return (w, lax.rem(y + t, p.ny) * 2 + c)

    def xb_copy(t):
        return copy_to(x_b.at[x], x_b.at[x], xb_s.at[t], xb_r.at[x], x_id(t))

    def xb_arrival(t):
        frm = lax.rem(x + t, p.nx)
        return copy_to(x_b.at[frm], x_b.at[frm], xb_s.at[0], xb_r.at[frm], x_id(t))

    def yb_copy(t):
        return copy_to(y_b.at[y], y_b.at[y], yb_s.at[t], yb_r.at[y], y_id(t))

    def yb_arrival(t):
        frm = lax.rem(y + t, p.ny)
        return copy_to(y_b.at[frm], y_b.at[frm], yb_s.at[0], yb_r.at[frm], y_id(t))

    def take(arrival, ref, turn):
        def body(t, total):
            arrival(t).wait_recv()
            return total + ref[turn(t)].astype(F32)

        return body

    def put_b(ref, at, total):
        ref[at, : p.rb, :] = total[: p.rb].astype(BF16)
        ref[at, p.rb :, :] = resplit(total[p.rb :], p.nb).astype(BF16)

    put_b(x_b, x, lax.fori_loop(1, p.nz, take(zb_arrival, z_b, along), chip_b[z].astype(F32)))
    each(p.nx, lambda t: xb_copy(t).start())
    total = lax.fori_loop(1, p.peers, take(xa_arrival, xy_a, plane), chip_a[q0].astype(F32))
    z_a[z] = total.astype(BF16)
    each(p.nz, lambda t: za_copy(t).start())
    put_b(y_b, y, lax.fori_loop(1, p.nx, take(xb_arrival, x_b, lambda t: lax.rem(x + t, p.nx)), x_b[x].astype(F32)))
    each(p.ny, lambda t: yb_copy(t).start())
    pending += [(p.nx, xb_copy), (p.nz, za_copy), (p.ny, yb_copy)]
    raw_start(2)

    def rows_a(q):
        return pl.ds(pl.multiple_of(q * p.ra, 16), p.ra)

    def rows_b(k):
        return pl.ds(pl.multiple_of(p.base + k * p.rb, 16), p.rb)

    def ga_copy(t):
        mine = agbuf.at[c, rows_a(q0), :]
        return copy_to(mine, mine, ga_s.at[t], ga_r.at[q0], plane_id(plane(t)))

    def ga_arrival(t):
        slot = agbuf.at[c, rows_a(plane(t)), :]
        return copy_to(slot, slot, ga_s.at[0], ga_r.at[plane(t)], plane_id(plane(t)))

    def gb_copy(t):
        mine = agbuf.at[c, rows_b(z), :]
        return copy_to(mine, mine, gb_s.at[t], gb_r.at[z], along_id(along(t)))

    def gb_arrival(t):
        slot = agbuf.at[c, rows_b(along(t)), :]
        return copy_to(slot, slot, gb_s.at[0], gb_r.at[along(t)], along_id(along(t)))

    def fa_copy(t):
        slot = agbuf.at[c, rows_a(plane(t)), :]
        return copy_to(slot, slot, fa_s.at[t], fa_r.at[plane(t)], sibling)

    def fb_copy(t):
        slot = agbuf.at[c, rows_b(along(t)), :]
        return copy_to(slot, slot, fb_s.at[t], fb_r.at[along(t)], sibling)

    def fa_arrival(q):
        slot = agbuf.at[1 - c, rows_a(q), :]
        return copy_to(slot, slot, fa_s.at[0], fa_r.at[q], sibling)

    def fb_arrival(k):
        slot = agbuf.at[1 - c, rows_b(k), :]
        return copy_to(slot, slot, fb_s.at[0], fb_r.at[k], sibling)

    total = lax.fori_loop(1, p.nz, take(za_arrival, z_a, along), z_a[z].astype(F32))
    agbuf[c, rows_a(q0), :] = total.astype(BF16)
    each(p.peers, lambda t: ga_copy(t).start())
    fa_copy(0).start()
    total = lax.fori_loop(1, p.ny, take(yb_arrival, y_b, lambda t: lax.rem(y + t, p.ny)), y_b[y].astype(F32))
    agbuf[c, rows_b(z), :] = total[: p.rb].astype(BF16)
    each(p.nz, lambda t: gb_copy(t).start())
    fb_copy(0).start()
    pending += [(p.peers, ga_copy), (p.nz, gb_copy), (p.peers, fa_copy), (p.nz, fb_copy), fa_copy(0), fb_copy(0)]
    raw_start(3)
    for i in range(p.nb):
        row = total[p.rb + i : p.rb + i + 1] + total[p.rb + p.nb + i : p.rb + p.nb + i + 1]
        prow[:, i * 128 : i * 128 + 128] = row

    def pass_a(t):
        ga_arrival(t).wait_recv()
        fa_copy(t).start()

    def pass_b(t):
        gb_arrival(t).wait_recv()
        fb_copy(t).start()

    each(p.nz, pass_b)
    each(p.peers, pass_a)
    raw_start(4)
    lax.fori_loop(0, p.nz, lambda k, carry: (fb_arrival(k).wait_recv(), carry)[1], 0)
    lax.fori_loop(0, p.peers, lambda q, carry: (fa_arrival(q).wait_recv(), carry)[1], 0)

    diag = lax.broadcasted_iota(jnp.int32, (128, 128), 0) == lax.broadcasted_iota(jnp.int32, (128, 128), 1)
    eye = diag.astype(F32)
    square = jnp.zeros((128, 128), F32)
    index = 0
    for i in range(p.nb):
        for j in range(i, p.nb):
            h, pos = divmod(index, p.half)
            block = agbuf[h, pos * 128 : pos * 128 + 128, :]
            wide = block.astype(F32)
            if i == j:
                wide = wide + eye
                block = wide.astype(BF16)
                square = square + wide * wide
            else:
                square = square + 2.0 * (wide * wide)
                gram[j * 128 : j * 128 + 128, i * 128 : i * 128 + 128] = wide.T.astype(BF16)
            gram[i * 128 : i * 128 + 128, j * 128 : j * 128 + 128] = block
            index += 1
    square = jnp.sum(jnp.sum(square, axis=0, keepdims=True), axis=1, keepdims=True)
    frob = jnp.sqrt(square)
    inv = 1.0 / frob

    strips = p.m // p.strip

    def mm(a, b):
        return jnp.dot(a, b, preferred_element_type=F32)

    def put(ref, s, value):
        cols = slice(s * p.strip, (s + 1) * p.strip)
        value = value.astype(ref.dtype)
        ref[: (s + 1) * p.strip, cols] = value
        if s > 0:
            ref[cols, : s * p.strip] = value[: s * p.strip].T

    def corner(s):
        return slice(0, (s + 1) * p.strip), slice(s * p.strip, (s + 1) * p.strip)

    for s in range(strips):
        rows, cols = corner(s)
        unit = gram[rows, cols].astype(F32) * inv
        unit2 = mm(gram[rows, :], gram[:, cols]) * (inv * inv)
        put(prod, s, unit2)
        put(mix, s, 0.0625 * unit2 - 0.5625 * unit)
        est[rows, cols] = 1.6875 * unit2 - 2.4375 * unit
    for s in range(strips):
        rows, cols = corner(s)
        new = est[rows, cols] + mm(prod[rows, :], mix[:, cols])
        est[rows, cols] = new
        put(estb, s, new)
    for s in range(strips):
        rows, cols = corner(s)
        half = gram[rows, cols].astype(F32) * (2.25 * inv) + mm(gram[rows, :], estb[:, cols]) * inv
        more[rows, cols] = half
        put(prod, s, half)
    for s in range(strips):
        rows, cols = corner(s)
        unit = 2.25 * more[rows, cols] + mm(prod[rows, :], estb[:, cols])
        more[rows, cols] = unit
        put(mix, s, unit)
    for s in range(strips):
        rows, cols = corner(s)
        unit = more[rows, cols]
        unit2 = mm(mix[rows, :], mix[:, cols])
        put(prod, s, unit2)
        put(moreb, s, 0.0625 * unit2 - 0.5625 * unit)
        more[rows, cols] = 1.6875 * unit2 - 2.4375 * unit
    for s in range(strips):
        rows, cols = corner(s)
        new = more[rows, cols] + mm(prod[rows, :], moreb[:, cols])
        put(mix, s, new)
        est[rows, cols] = 2.25 * (est[rows, cols] + new)
    for s in range(strips):
        rows, cols = corner(s)
        new = est[rows, cols] + mm(estb[rows, :], mix[:, cols])
        row_ids = lax.broadcasted_iota(jnp.int32, new.shape, 0)
        col_ids = lax.broadcasted_iota(jnp.int32, new.shape, 1) + s * p.strip
        put(est, s, new + jnp.where(row_ids == col_ids, 2.25 * 2.25, 0.0))

    inv_root = lax.rsqrt(frob)

    def shift_rows(s, total):
        rows = pl.ds(pl.multiple_of(s * 128, 128), 128)
        block = est[rows, :]
        midway = jnp.sum(block * prow[...], axis=1, keepdims=True)
        return total + jnp.sum(block * midway, axis=0, keepdims=True)

    shift = lax.fori_loop(0, p.m // 128, shift_rows, jnp.zeros((1, p.m), F32))
    shift = shift * (inv / root_scale)

    def transform_rows(s, carry):
        rows = pl.ds(pl.multiple_of(s * 128, 128), 128)
        tmat[rows, :] = (est[rows, :] * inv_root + shift).astype(BF16)
        return carry

    lax.fori_loop(0, p.m // 128, transform_rows, 0)

    for k in p.near:
        raw_arrival(k, 0).wait_recv()
        raw_arrival(k, 1).wait_recv()
    own.wait()
    state_mean = jnp.zeros((1, p.share), F32)
    for k in range(p.narrow):
        state_mean = state_mean + jnp.sum(raw[k].astype(F32), axis=0, keepdims=True)
    state_mean = state_mean / p.m
    factors = [
        jnp.full((1, 128), infl[owner[n * (p.share // 128) + b]], F32) for b in range(p.share // 128)
    ]
    factors = jnp.concatenate(factors, axis=1)
    for k in range(p.narrow):
        anom[k * 128 : k * 128 + 128, :] = (factors * (raw[k].astype(F32) - state_mean)).astype(BF16)

    def out_copy(dy, core):
        there = lax.rem(y + dy, p.ny) * 2 + core
        return copy_to(
            stage.at[dy, pl.ds(core * 128, 128), :], out.at[:, share_cols(n)], out_s.at[dy, core],
            out_r.at[n], (w, there)
        )

    def out_arrival(frm):
        return copy_to(
            stage.at[0, pl.ds(0, 128), :], out.at[:, share_cols(frm)], out_s.at[0, 0], out_r.at[frm], (w, frm)
        )

    def analyse(dy):
        rows = pl.ds(pl.multiple_of(lax.rem(y + dy, p.ny) * 256, 256), 256)
        stage[dy] = (state_mean + mm(tmat[rows, :], anom[...])).astype(BF16)

    order = sorted(range(1, p.ny), key=lambda d: -min(d, p.ny - d))
    for dy in order:
        analyse(dy)
        for core in range(2):
            out_copy(dy, core).start()
    analyse(0)
    to_sibling = copy_to(
        stage.at[0, pl.ds(pl.multiple_of((1 - c) * 128, 128), 128), :], out.at[:, share_cols(n)], out_s.at[0, 0], out_r.at[n], sibling
    )
    to_sibling.start()
    keep = pltpu.make_async_copy(
        stage.at[0, pl.ds(pl.multiple_of(c * 128, 128), 128), :], out.at[:, share_cols(n)], own_sem
    )
    keep.start()

    for k in p.near:
        out_arrival(near(k)).wait_recv()
    keep.wait()
    pending.append(to_sibling)
    pending += [out_copy(dy, core) for dy in order for core in range(2)]
    finish(pending)


def on_device(grid, narrow, ensemble, owner, inflation, obs_block, obs_value, obs_std):
    p = Plan(grid, narrow, *ensemble.shape, obs_value.shape[0])
    dma = pltpu.SemaphoreType.DMA
    vmem, smem = pl.BlockSpec(memory_space=pltpu.VMEM), pl.BlockSpec(memory_space=pltpu.SMEM)
    anywhere = pl.BlockSpec(memory_space=pl.ANY)
    square = (p.m, p.m)
    scratch = [
        pltpu.VMEM((p.states // 128, p.ml, 128), BF16),
        pltpu.VMEM((p.narrow, p.ml, p.oshare), BF16),
        pltpu.VMEM((p.narrow, p.ml, p.oshare), BF16),
        pltpu.VMEM((p.m, p.oshare), BF16),
        pltpu.VMEM((2, p.peers, p.ra, 128), BF16),
        pltpu.VMEM((2, p.nz, p.tb, 128), BF16),
        pltpu.VMEM((p.peers, p.ra, 128), BF16),
        pltpu.VMEM((p.nz, p.tb, 128), BF16),
        pltpu.VMEM((p.peers, p.ra, 128), BF16),
        pltpu.VMEM((p.nz, p.tb, 128), BF16),
        pltpu.VMEM((p.peers, p.ra, 128), BF16),
        pltpu.VMEM((p.nz, p.tb, 128), BF16),
        pltpu.VMEM((p.nz, p.ra, 128), BF16),
        pltpu.VMEM((p.nx, p.tb, 128), BF16),
        pltpu.VMEM((p.ny, p.tb, 128), BF16),
        pltpu.VMEM((16, 128), F32),
        pltpu.VMEM((1, p.m), F32),
        pltpu.VMEM((2, p.half * 128, 128), BF16),
        pltpu.VMEM(square, BF16),
        pltpu.VMEM(square, BF16),
        pltpu.VMEM(square, BF16),
        pltpu.VMEM(square, F32),
        pltpu.VMEM(square, BF16),
        pltpu.VMEM(square, F32),
        pltpu.VMEM(square, BF16),
        pltpu.VMEM((p.narrow, p.ml, p.share), BF16),
        pltpu.VMEM((p.m, p.share), BF16),
        pltpu.VMEM(square, BF16),
        pltpu.VMEM((p.ny, 256, p.share), BF16),
        dma, dma((p.narrow,)), dma((p.narrow,)),
        dma((2,)), dma((2,)),
        dma((p.peers,)), dma((p.peers,)), dma((p.nz,)), dma((p.nz,)),
        dma((p.nz,)), dma((p.nz,)), dma((p.nx,)), dma((p.nx,)), dma((p.ny,)), dma((p.ny,)),
        dma((p.peers,)), dma((p.peers,)), dma((p.nz,)), dma((p.nz,)),
        dma((p.peers,)), dma((p.peers,)), dma((p.nz,)), dma((p.nz,)),
        dma((p.narrow, 2)), dma((p.narrow, 2)),
        dma, dma((p.ny, 2)), dma((p.narrow,)),
    ]
    return pl.pallas_call(
        functools.partial(kernel, p),
        out_shape=jax.ShapeDtypeStruct(ensemble.shape, BF16),
        in_specs=[smem, smem, smem, anywhere, vmem, vmem],
        out_specs=anywhere,
        scratch_shapes=scratch,
        compiler_params=pltpu.CompilerParams(
            collective_id=0, has_side_effects=True, vmem_limit_bytes=56 * 1024 * 1024
        ),
        name="etkf",
    )(owner, inflation, obs_block, ensemble, obs_value.reshape(-1, 128), obs_std.reshape(-1, 128))


def solution(mesh):
    wide, narrow = mesh.shape["wide"], mesh.shape["narrow"]
    grid = (4, wide // 4) if wide >= 16 else (2, wide // 2)
    return jax.shard_map(
        functools.partial(on_device, grid, narrow),
        mesh=mesh,
        in_specs=(P("narrow", "wide"), P("wide"), P(), P("wide"), P("wide"), P("wide")),
        out_specs=P("narrow", "wide"),
        check_vma=False,
    )
```

```python
import functools
import math

import jax
import jax.numpy as jnp
from jax import lax
from jax.experimental import pallas as pl
from jax.experimental.pallas import tpu as pltpu
from jax.sharding import PartitionSpec as P

CLASSES = 128
MESH = pl.DeviceIdType.MESH
F32 = jnp.float32
BF16 = jnp.bfloat16
NT = (((1,), (1,)), ((), ()))
RAW_AT = ((None, None, 0, 0), (4, 4, 4, 4), (0, 2, 1, 4))


class Plan:
    def __init__(self, grid, narrow, local_members, local_states, obs_local):
        self.nx, self.nz = grid
        self.narrow = narrow
        self.ny = narrow // 2
        self.ml = local_members
        self.m = local_members * narrow
        self.states = local_states
        self.share = local_states // narrow
        self.obs = obs_local
        self.oshare = obs_local // narrow
        self.nb = self.m // 128
        self.blocks = [(i, j) for i in range(self.nb) for j in range(i, self.nb)]
        self.half = len(self.blocks) // 2
        self.peers = self.nx * self.ny
        tiles = self.half * 8
        self.ra = tiles * 2 // 3 // self.peers * 16
        self.rb = (tiles * 16 - self.ra * self.peers) // self.nz
        self.tb = self.rb + 16
        self.base = self.ra * self.peers
        self.strip = min(256, self.m)
        assert self.half * 2 == len(self.blocks) and self.rb % 16 == 0
        assert local_members == 128 and self.base + self.rb * self.nz == self.half * 128
        self.near = sorted(((d, f) for d in range(self.ny) for f in range(2) if d + f), key=lambda k: -min(k[0], self.ny - k[0]))


def segments(plan, pos):
    out, row = [], pos * 128
    while row < (pos + 1) * 128:
        first = row < plan.base
        size = plan.ra if first else plan.rb
        piece, inside = divmod(row if first else row - plan.base, size)
        count = min(size - inside, (pos + 1) * 128 - row)
        out.append((first, piece, inside, row - pos * 128, count))
        row += count
    return out


def resplit(tail, nb):
    total = tail[:nb] + tail[nb : 2 * nb]
    high = total.astype(BF16).astype(F32)
    rest = [high, total - high]
    if 2 * nb < 16:
        rest.append(jnp.zeros((16 - 2 * nb, 128), F32))
    return jnp.concatenate(rest, axis=0)


def kernel(plan, owner, infl, oblk, ens, value, std, out, ens_v, gat, robs, scaled, part_a, part_b, core_a, core_b, chip_a,
           chip_b, xy_a, z_b, z_a, x_b, y_b, tailbuf, prow, agbuf, gram, prod, mix, est, estb, more, moreb, raw, anom, tmat, stage,
           load_sem, obs_s, obs_r, core_s, core_r, xa_s, xa_r, zb_s, zb_r, za_s, za_r, xb_s, xb_r, yb_s, yb_r, ga_s, ga_r, gb_s, gb_r,
           fa_s, fa_r, fb_s, fb_r, raw_s, raw_r, own_sem, out_s, out_r):
    p = plan
    n = lax.axis_index("narrow")
    w = lax.axis_index("wide")
    x, z = lax.div(w, p.nz), lax.rem(w, p.nz)
    y, c = lax.div(n, 2), lax.rem(n, 2)
    q0 = x * p.ny + y
    root_scale = math.sqrt(p.m - 1)
    pending = []

    def copy_to(src, dst, send, recv, device):
        return pltpu.make_async_remote_copy(
            src_ref=src, dst_ref=dst, send_sem=send, recv_sem=recv, device_id=device, device_id_type=MESH
        )

    def near(k):
        return lax.rem(y + k[0], p.ny) * 2 + (1 - c if k[1] else c)

    def along(t):
        return lax.rem(z + t, p.nz)

    def along_id(k):
        return (x * p.nz + k, n)

    def plane(t):
        return lax.rem(q0 + t, p.peers)

    def plane_id(q):
        return (lax.div(q, p.ny) * p.nz + z, lax.rem(q, p.ny) * 2 + c)

    sibling = (w, n + 1 - 2 * c)

    def each(count, step):
        def body(t, carry):
            step(t)
            return carry

        lax.fori_loop(1, count, body, 0)

    def finish(items):
        for item in items:
            if isinstance(item, tuple):
                each(item[0], lambda t: item[1](t).wait_send())
            else:
                item.wait_send()

    def load_block(b):
        cols = pl.ds(pl.multiple_of(b * 128, 128), 128)
        return pltpu.make_async_copy(ens.at[:, cols], ens_v.at[b], load_sem)

    barrier = pltpu.get_barrier_semaphore()
    greeted = 0
    for k in p.near:
        pl.semaphore_signal(barrier, inc=1, device_id=(w, near(k)), device_id_type=MESH)
        greeted += 1
    lax.fori_loop(0, p.states // 128, lambda b, carry: (load_block(b).start(), carry)[1], 0)
    for t in range(1, p.nz):
        pl.semaphore_signal(barrier, inc=1, device_id=along_id(along(t)), device_id_type=MESH)
        greeted += 1
    for dx in range(1, p.nx):
        for dy in range(p.ny):
            there = (lax.rem(x + dx, p.nx) * p.nz + z, lax.rem(y + dy, p.ny) * 2 + c)
            pl.semaphore_signal(barrier, inc=1, device_id=there, device_id_type=MESH)
            greeted += 1

    pltpu.make_async_copy(ens_v, ens_v, load_sem).wait()
    per = p.oshare // 128
    for b in range(p.obs // 128):
        gat[b // per, :, (b % per) * 128 : (b % per) * 128 + 128] = ens_v[oblk[b]]
    pl.semaphore_wait(barrier, greeted)

    def obs_copy(k):
        there = near(k)
        return copy_to(gat.at[there], robs.at[n], obs_s.at[2 * k[0] + k[1]], obs_r.at[n], (w, there))

    def obs_arrival(k):
        frm = near(k)
        return copy_to(gat.at[frm], robs.at[frm], obs_s.at[0], obs_r.at[frm], (w, frm))

    for k in p.near:
        obs_copy(k).start()
        pending.append(obs_copy(k))
    robs[pl.ds(n, 1)] = gat[pl.ds(n, 1)]
    for k in p.near:
        obs_arrival(k).wait_recv()

    def share_cols(k):
        return pl.ds(pl.multiple_of(k * p.share, 128), p.share)

    def half_cols(k, h):
        return pl.ds(pl.multiple_of(k * p.share + h * (p.share // 2), 128), p.share // 2)

    def half_slot(k, h):
        return raw.at[k, :, pl.ds(h * (p.share // 2), p.share // 2)]

    def raw_copy(k, h):
        there = near(k)
        src = ens.at[:, half_cols(there, h)]
        return copy_to(src, half_slot(n, h), raw_s.at[2 * k[0] + k[1], h], raw_r.at[n, h], (w, there))

    def raw_arrival(k, h):
        frm = near(k)
        return copy_to(ens.at[:, half_cols(frm, h)], half_slot(frm, h), raw_s.at[0, 0], raw_r.at[frm, h], (w, frm))

    def raw_start(when):
        for h in range(2):
            for k in p.near:
                if RAW_AT[min(k[0], p.ny - k[0])][2 * k[1] + h] == when:
                    raw_copy(k, h).start()
                    pending.append(raw_copy(k, h))

    own = pltpu.make_async_copy(ens.at[:, share_cols(n)], raw.at[n], own_sem.at[0])
    own.start()
    raw_start(0)

    innov = []
    for k in range(per):
        cols = slice(k * 128, k * 128 + 128)
        member = robs[:, :, cols].reshape(p.m, 128).astype(F32)
        mean = jnp.sum(member, axis=0, keepdims=True) / p.m
        ob = n * per + k
        factor = infl[owner[oblk[ob]]]
        sigma = std[pl.ds(ob, 1), :]
        shifted = (factor * (member - mean)).astype(BF16)
        scaled[:, cols] = (shifted.astype(F32) / (sigma * root_scale)).astype(BF16)
        innov.append((value[pl.ds(ob, 1), :] - mean) / sigma)
    innov = jnp.concatenate(innov, axis=1)
    high = innov.astype(BF16).astype(F32)
    middle = (innov - high).astype(BF16).astype(F32)
    low = innov - high - middle
    row_ids = lax.broadcasted_iota(jnp.int32, (16, p.oshare), 0)
    lhs = jnp.where(row_ids == 0, high, jnp.where(row_ids == 1, middle, jnp.where(row_ids == 2, low, 0.0)))
    projected = lax.dot_general(lhs.astype(BF16), scaled[...], NT, preferred_element_type=F32)
    projected = jnp.sum(projected, axis=0, keepdims=True)
    tailbuf[...] = jnp.zeros_like(tailbuf)
    for i in range(p.nb):
        tailbuf[i : i + 1, :] = projected[:, i * 128 : i * 128 + 128]
    tail = resplit(tailbuf[...], p.nb).astype(BF16)
    for h in range(2):
        part_b[h, 0, p.rb :, :] = tail
        for k in range(1, p.nz):
            part_b[h, k, p.rb :, :] = jnp.zeros_like(tail)
    index = 0
    for i in range(p.nb):
        rows = lax.dot_general(
            scaled[i * 128 : i * 128 + 128, :], scaled[i * 128 :, :], NT, preferred_element_type=F32
        ).astype(BF16)
        for j in range(i, p.nb):
            h, pos = divmod(index, p.half)
            for first, piece, inside, start, count in segments(p, pos):
                ref = part_a if first else part_b
                ref[h, piece, inside : inside + count, :] = rows[start : start + count, (j - i) * 128 : (j - i) * 128 + 128]
            index += 1

    core_copy_b = copy_to(part_b.at[1 - c], core_b, core_s.at[0], core_r.at[0], sibling)
    core_copy_a = copy_to(part_a.at[1 - c], core_a, core_s.at[1], core_r.at[1], sibling)
    core_copy_b.start()
    core_copy_a.start()
    pending += [core_copy_a, core_copy_b]

    def zb_copy(t):
        there = along(t)
        return copy_to(chip_b.at[there], z_b.at[z], zb_s.at[t], zb_r.at[z], along_id(there))

    def zb_arrival(t):
        frm = along(t)
        return copy_to(chip_b.at[frm], z_b.at[frm], zb_s.at[0], zb_r.at[frm], along_id(frm))

    def xa_copy(t):
        there = plane(t)
        return copy_to(chip_a.at[there], xy_a.at[q0], xa_s.at[t], xa_r.at[q0], plane_id(there))

    def xa_arrival(t):
        frm = plane(t)
        return copy_to(chip_a.at[frm], xy_a.at[frm], xa_s.at[0], xa_r.at[frm], plane_id(frm))

    def add_b(k, carry):
        total = part_b[c, k, : p.rb, :].astype(F32) + core_b[k, : p.rb, :].astype(F32)
        chip_b[k, : p.rb, :] = total.astype(BF16)
        chip_b[k, p.rb :, :] = tail
        return carry

    def add_a(k, carry):
        chip_a[k] = (part_a[c, k].astype(F32) + core_a[k].astype(F32)).astype(BF16)
        return carry

    core_copy_b.wait_recv()
    tail = resplit(part_b[c, 0, p.rb :, :].astype(F32) + core_b[0, p.rb :, :].astype(F32), p.nb).astype(BF16)
    lax.fori_loop(0, p.nz, add_b, 0)
    each(p.nz, lambda t: zb_copy(t).start())
    core_copy_a.wait_recv()
    lax.fori_loop(0, p.peers, add_a, 0)
    each(p.peers, lambda t: xa_copy(t).start())
    pending += [(p.nz, zb_copy), (p.peers, xa_copy)]
    raw_start(1)

    def za_copy(t):
        return copy_to(z_a.at[z], z_a.at[z], za_s.at[t], za_r.at[z], along_id(along(t)))

    def za_arrival(t):
        frm = along(t)
        return copy_to(z_a.at[frm], z_a.at[frm], za_s.at[0], za_r.at[frm], along_id(frm))

    def x_id(t):
        return (lax.rem(x + t, p.nx) * p.nz + z, n)

    def y_id(t):
        return (w, lax.rem(y + t, p.ny) * 2 + c)

    def xb_copy(t):
        return copy_to(x_b.at[x], x_b.at[x], xb_s.at[t], xb_r.at[x], x_id(t))

    def xb_arrival(t):
        frm = lax.rem(x + t, p.nx)
        return copy_to(x_b.at[frm], x_b.at[frm], xb_s.at[0], xb_r.at[frm], x_id(t))

    def yb_copy(t):
        return copy_to(y_b.at[y], y_b.at[y], yb_s.at[t], yb_r.at[y], y_id(t))

    def yb_arrival(t):
        frm = lax.rem(y + t, p.ny)
        return copy_to(y_b.at[frm], y_b.at[frm], yb_s.at[0], yb_r.at[frm], y_id(t))

    def take(arrival, ref, turn):
        def body(t, total):
            arrival(t).wait_recv()
            return total + ref[turn(t)].astype(F32)

        return body

    def put_b(ref, at, total):
        ref[at, : p.rb, :] = total[: p.rb].astype(BF16)
        ref[at, p.rb :, :] = resplit(total[p.rb :], p.nb).astype(BF16)

    put_b(x_b, x, lax.fori_loop(1, p.nz, take(zb_arrival, z_b, along), chip_b[z].astype(F32)))
    each(p.nx, lambda t: xb_copy(t).start())
    total = lax.fori_loop(1, p.peers, take(xa_arrival, xy_a, plane), chip_a[q0].astype(F32))
    z_a[z] = total.astype(BF16)
    each(p.nz, lambda t: za_copy(t).start())
    put_b(y_b, y, lax.fori_loop(1, p.nx, take(xb_arrival, x_b, lambda t: lax.rem(x + t, p.nx)), x_b[x].astype(F32)))
    each(p.ny, lambda t: yb_copy(t).start())
    pending += [(p.nx, xb_copy), (p.nz, za_copy), (p.ny, yb_copy)]
    raw_start(2)

    def rows_a(q):
        return pl.ds(pl.multiple_of(q * p.ra, 16), p.ra)

    def rows_b(k):
        return pl.ds(pl.multiple_of(p.base + k * p.rb, 16), p.rb)

    def ga_copy(t):
        mine = agbuf.at[c, rows_a(q0), :]
        return copy_to(mine, mine, ga_s.at[t], ga_r.at[q0], plane_id(plane(t)))

    def ga_arrival(t):
        slot = agbuf.at[c, rows_a(plane(t)), :]
        return copy_to(slot, slot, ga_s.at[0], ga_r.at[plane(t)], plane_id(plane(t)))

    def gb_copy(t):
        mine = agbuf.at[c, rows_b(z), :]
        return copy_to(mine, mine, gb_s.at[t], gb_r.at[z], along_id(along(t)))

    def gb_arrival(t):
        slot = agbuf.at[c, rows_b(along(t)), :]
        return copy_to(slot, slot, gb_s.at[0], gb_r.at[along(t)], along_id(along(t)))

    def fa_copy(t):
        slot = agbuf.at[c, rows_a(plane(t)), :]
        return copy_to(slot, slot, fa_s.at[t], fa_r.at[plane(t)], sibling)

    def fb_copy(t):
        slot = agbuf.at[c, rows_b(along(t)), :]
        return copy_to(slot, slot, fb_s.at[t], fb_r.at[along(t)], sibling)

    def fa_arrival(q):
        slot = agbuf.at[1 - c, rows_a(q), :]
        return copy_to(slot, slot, fa_s.at[0], fa_r.at[q], sibling)

    def fb_arrival(k):
        slot = agbuf.at[1 - c, rows_b(k), :]
        return copy_to(slot, slot, fb_s.at[0], fb_r.at[k], sibling)

    total = lax.fori_loop(1, p.nz, take(za_arrival, z_a, along), z_a[z].astype(F32))
    agbuf[c, rows_a(q0), :] = total.astype(BF16)
    each(p.peers, lambda t: ga_copy(t).start())
    fa_copy(0).start()
    total = lax.fori_loop(1, p.ny, take(yb_arrival, y_b, lambda t: lax.rem(y + t, p.ny)), y_b[y].astype(F32))
    agbuf[c, rows_b(z), :] = total[: p.rb].astype(BF16)
    each(p.nz, lambda t: gb_copy(t).start())
    fb_copy(0).start()
    pending += [(p.peers, ga_copy), (p.nz, gb_copy), (p.peers, fa_copy), (p.nz, fb_copy), fa_copy(0), fb_copy(0)]
    raw_start(3)
    for i in range(p.nb):
        row = total[p.rb + i : p.rb + i + 1] + total[p.rb + p.nb + i : p.rb + p.nb + i + 1]
        prow[:, i * 128 : i * 128 + 128] = row

    def pass_a(t):
        ga_arrival(t).wait_recv()
        fa_copy(t).start()

    def pass_b(t):
        gb_arrival(t).wait_recv()
        fb_copy(t).start()

    each(p.nz, pass_b)
    each(p.peers, pass_a)
    raw_start(4)
    lax.fori_loop(0, p.nz, lambda k, carry: (fb_arrival(k).wait_recv(), carry)[1], 0)
    lax.fori_loop(0, p.peers, lambda q, carry: (fa_arrival(q).wait_recv(), carry)[1], 0)

    diag = lax.broadcasted_iota(jnp.int32, (128, 128), 0) == lax.broadcasted_iota(jnp.int32, (128, 128), 1)
    eye = diag.astype(F32)
    square = jnp.zeros((128, 128), F32)
    index = 0
    for i in range(p.nb):
        for j in range(i, p.nb):
            h, pos = divmod(index, p.half)
            block = agbuf[h, pos * 128 : pos * 128 + 128, :]
            wide = block.astype(F32)
            if i == j:
                wide = wide + eye
                block = wide.astype(BF16)
                square = square + wide * wide
            else:
                square = square + 2.0 * (wide * wide)
                gram[j * 128 : j * 128 + 128, i * 128 : i * 128 + 128] = wide.T.astype(BF16)
            gram[i * 128 : i * 128 + 128, j * 128 : j * 128 + 128] = block
            index += 1
    square = jnp.sum(jnp.sum(square, axis=0, keepdims=True), axis=1, keepdims=True)
    frob = jnp.sqrt(square)
    inv = 1.0 / frob

    strips = p.m // p.strip

    def mm(a, b):
        return jnp.dot(a, b, preferred_element_type=F32)

    def put(ref, s, value):
        cols = slice(s * p.strip, (s + 1) * p.strip)
        value = value.astype(ref.dtype)
        ref[: (s + 1) * p.strip, cols] = value
        if s > 0:
            ref[cols, : s * p.strip] = value[: s * p.strip].T

    def corner(s):
        return slice(0, (s + 1) * p.strip), slice(s * p.strip, (s + 1) * p.strip)

    for s in reversed(range(strips)):
        rows, cols = corner(s)
        unit = gram[rows, cols].astype(F32) * inv
        unit2 = mm(gram[rows, :], gram[:, cols]) * (inv * inv)
        put(prod, s, unit2)
        put(mix, s, 0.0625 * unit2 - 0.5625 * unit)
        est[rows, cols] = 1.6875 * unit2 - 2.4375 * unit
    for s in reversed(range(strips)):
        rows, cols = corner(s)
        new = est[rows, cols] + mm(prod[rows, :], mix[:, cols])
        est[rows, cols] = new
        put(estb, s, new)
    for s in reversed(range(strips)):
        rows, cols = corner(s)
        half = gram[rows, cols].astype(F32) * (2.25 * inv) + mm(gram[rows, :], estb[:, cols]) * inv
        more[rows, cols] = half
        put(prod, s, half)
    for s in reversed(range(strips)):
        rows, cols = corner(s)
        unit = 2.25 * more[rows, cols] + mm(prod[rows, :], estb[:, cols])
        more[rows, cols] = unit
        put(mix, s, unit)
    for s in reversed(range(strips)):
        rows, cols = corner(s)
        unit = more[rows, cols]
        unit2 = mm(mix[rows, :], mix[:, cols])
        put(prod, s, unit2)
        put(moreb, s, 0.0625 * unit2 - 0.5625 * unit)
        more[rows, cols] = 1.6875 * unit2 - 2.4375 * unit
    for s in reversed(range(strips)):
        rows, cols = corner(s)
        new = more[rows, cols] + mm(prod[rows, :], moreb[:, cols])
        put(mix, s, new)
        est[rows, cols] = 2.25 * (est[rows, cols] + new)
    for s in reversed(range(strips)):
        rows, cols = corner(s)
        new = est[rows, cols] + mm(estb[rows, :], mix[:, cols])
        row_ids = lax.broadcasted_iota(jnp.int32, new.shape, 0)
        col_ids = lax.broadcasted_iota(jnp.int32, new.shape, 1) + s * p.strip
        put(est, s, new + jnp.where(row_ids == col_ids, 2.25 * 2.25, 0.0))

    inv_root = lax.rsqrt(frob)

    def shift_rows(s, total):
        rows = pl.ds(pl.multiple_of(s * 128, 128), 128)
        block = est[rows, :]
        midway = jnp.sum(block * prow[...], axis=1, keepdims=True)
        return total + jnp.sum(block * midway, axis=0, keepdims=True)

    shift = lax.fori_loop(0, p.m // 128, shift_rows, jnp.zeros((1, p.m), F32))
    shift = shift * (inv / root_scale)

    def transform_rows(s, carry):
        rows = pl.ds(pl.multiple_of(s * 128, 128), 128)
        tmat[rows, :] = (est[rows, :] * inv_root + shift).astype(BF16)
        return carry

    lax.fori_loop(0, p.m // 128, transform_rows, 0)

    per_half = p.share // 2

    def out_copy(dy, core, h):
        there = lax.rem(y + dy, p.ny) * 2 + core
        cols = pl.ds(h * per_half, per_half)
        return copy_to(
            stage.at[dy, pl.ds(core * 128, 128), cols], out.at[:, half_cols(n, h)], out_s.at[dy, core, h], out_r.at[n, h], (w, there)
        )

    def out_arrival(k, h):
        cols = pl.ds(h * per_half, per_half)
        slot = out.at[:, half_cols(near(k), h)]
        return copy_to(stage.at[0, pl.ds(0, 128), cols], slot, out_s.at[0, 0, h], out_r.at[near(k), h], (w, near(k)))

    def analyse(dy, h, mean):
        rows = pl.ds(pl.multiple_of(lax.rem(y + dy, p.ny) * 256, 256), 256)
        cols = slice(h * per_half, (h + 1) * per_half)
        stage[dy, :, cols] = (mean + mm(tmat[rows, :], anom[:, cols])).astype(BF16)

    order = sorted(range(1, p.ny), key=lambda d: -min(d, p.ny - d))
    means = []
    for h in range(2):
        for k in p.near:
            raw_arrival(k, h).wait_recv()
        if h == 0:
            own.wait()
        cols = slice(h * per_half, (h + 1) * per_half)
        mean = jnp.zeros((1, per_half), F32)
        for k in range(p.narrow):
            mean = mean + jnp.sum(raw[k, :, cols].astype(F32), axis=0, keepdims=True)
        mean = mean / p.m
        means.append(mean)
        first = n * (p.share // 128) + h * (per_half // 128)
        factors = [jnp.full((1, 128), infl[owner[first + b]], F32) for b in range(per_half // 128)]
        factors = jnp.concatenate(factors, axis=1)
        for k in range(p.narrow):
            anom[k * 128 : k * 128 + 128, cols] = (factors * (raw[k, :, cols].astype(F32) - mean)).astype(BF16)
        for dy in order:
            analyse(dy, h, mean)
            for core in range(2):
                out_copy(dy, core, h).start()
                pending.append(out_copy(dy, core, h))
    for h in range(2):
        analyse(0, h, means[h])
    rest = []
    for h in range(2):
        cols = pl.ds(h * per_half, per_half)
        theirs = stage.at[0, pl.ds(pl.multiple_of((1 - c) * 128, 128), 128), cols]
        mine = stage.at[0, pl.ds(pl.multiple_of(c * 128, 128), 128), cols]
        to_sibling = copy_to(theirs, out.at[:, half_cols(n, h)], out_s.at[0, 0, h], out_r.at[n, h], sibling)
        to_sibling.start()
        pending.append(to_sibling)
        keep = pltpu.make_async_copy(mine, out.at[:, half_cols(n, h)], own_sem.at[h])
        keep.start()
        rest.append(keep)
    for h in range(2):
        for k in p.near:
            out_arrival(k, h).wait_recv()
    for keep in rest:
        keep.wait()
    finish(pending)


def hand_on(parts, done, out, hold, in_sems, out_sems):
    rows = [pl.ds(k * (done.shape[0] // parts), done.shape[0] // parts) for k in range(parts)]
    reads = [pltpu.make_async_copy(done.at[r], hold.at[r], in_sems.at[k]) for k, r in enumerate(rows)]
    writes = [pltpu.make_async_copy(hold.at[r], out.at[r], out_sems.at[k]) for k, r in enumerate(rows)]
    for read in reads:
        read.start()
    for read, write in zip(reads, writes):
        read.wait()
        write.start()
    for write in writes:
        write.wait()


def on_device(grid, narrow, ensemble, owner, inflation, obs_block, obs_value, obs_std):
    p = Plan(grid, narrow, *ensemble.shape, obs_value.shape[0])
    dma = pltpu.SemaphoreType.DMA
    vmem, smem = pl.BlockSpec(memory_space=pltpu.VMEM), pl.BlockSpec(memory_space=pltpu.SMEM)
    anywhere = pl.BlockSpec(memory_space=pl.ANY)
    square = (p.m, p.m)
    scratch = [
        pltpu.VMEM((p.states // 128, p.ml, 128), BF16),
        pltpu.VMEM((p.narrow, p.ml, p.oshare), BF16),
        pltpu.VMEM((p.narrow, p.ml, p.oshare), BF16),
        pltpu.VMEM((p.m, p.oshare), BF16),
        pltpu.VMEM((2, p.peers, p.ra, 128), BF16),
        pltpu.VMEM((2, p.nz, p.tb, 128), BF16),
        pltpu.VMEM((p.peers, p.ra, 128), BF16),
        pltpu.VMEM((p.nz, p.tb, 128), BF16),
        pltpu.VMEM((p.peers, p.ra, 128), BF16),
        pltpu.VMEM((p.nz, p.tb, 128), BF16),
        pltpu.VMEM((p.peers, p.ra, 128), BF16),
        pltpu.VMEM((p.nz, p.tb, 128), BF16),
        pltpu.VMEM((p.nz, p.ra, 128), BF16),
        pltpu.VMEM((p.nx, p.tb, 128), BF16),
        pltpu.VMEM((p.ny, p.tb, 128), BF16),
        pltpu.VMEM((16, 128), F32),
        pltpu.VMEM((1, p.m), F32),
        pltpu.VMEM((2, p.half * 128, 128), BF16),
        pltpu.VMEM(square, BF16),
        pltpu.VMEM(square, BF16),
        pltpu.VMEM(square, BF16),
        pltpu.VMEM(square, F32),
        pltpu.VMEM(square, BF16),
        pltpu.VMEM(square, F32),
        pltpu.VMEM(square, BF16),
        pltpu.VMEM((p.narrow, p.ml, p.share), BF16),
        pltpu.VMEM((p.m, p.share), BF16),
        pltpu.VMEM(square, BF16),
        pltpu.VMEM((p.ny, 256, p.share), BF16),
        dma, dma((p.narrow,)), dma((p.narrow,)),
        dma((2,)), dma((2,)),
        dma((p.peers,)), dma((p.peers,)), dma((p.nz,)), dma((p.nz,)),
        dma((p.nz,)), dma((p.nz,)), dma((p.nx,)), dma((p.nx,)), dma((p.ny,)), dma((p.ny,)),
        dma((p.peers,)), dma((p.peers,)), dma((p.nz,)), dma((p.nz,)),
        dma((p.peers,)), dma((p.peers,)), dma((p.nz,)), dma((p.nz,)),
        dma((p.narrow, 2)), dma((p.narrow, 2)),
        dma((2,)), dma((p.ny, 2, 2)), dma((p.narrow, 2)),
    ]
    done = pl.pallas_call(
        functools.partial(kernel, p),
        out_shape=jax.ShapeDtypeStruct(ensemble.shape, BF16),
        in_specs=[smem, smem, smem, anywhere, vmem, vmem],
        out_specs=anywhere,
        scratch_shapes=scratch,
        compiler_params=pltpu.CompilerParams(
            collective_id=0, has_side_effects=True, vmem_limit_bytes=56 * 1024 * 1024
        ),
        name="etkf",
    )(owner, inflation, obs_block, ensemble, obs_value.reshape(-1, 128), obs_std.reshape(-1, 128))
    parts = p.ml // 16
    return pl.pallas_call(
        functools.partial(hand_on, parts),
        out_shape=jax.ShapeDtypeStruct(ensemble.shape, BF16),
        in_specs=[anywhere],
        out_specs=anywhere,
        scratch_shapes=[pltpu.VMEM(ensemble.shape, BF16), dma((parts,)), dma((parts,))],
        compiler_params=pltpu.CompilerParams(vmem_limit_bytes=56 * 1024 * 1024),
        name="hand_on",
    )(done)


def solution(mesh):
    wide, narrow = mesh.shape["wide"], mesh.shape["narrow"]
    grid = (4, wide // 4) if wide >= 16 else (2, wide // 2)
    return jax.shard_map(
        functools.partial(on_device, grid, narrow),
        mesh=mesh,
        in_specs=(P("narrow", "wide"), P("wide"), P(), P("wide"), P("wide"), P("wide")),
        out_specs=P("narrow", "wide"),
        check_vma=False,
    )
```

```python
import functools
import math

import jax
import jax.numpy as jnp
from jax import lax
from jax.experimental import pallas as pl
from jax.experimental.pallas import tpu as pltpu
from jax.sharding import PartitionSpec as P

CLASSES = 128
MESH = pl.DeviceIdType.MESH
F32 = jnp.float32
BF16 = jnp.bfloat16
NT = (((1,), (1,)), ((), ()))
RAW_AT = ((None, None, 0, 0), (4, 4, 4, 4), (0, 2, 1, 4))


class Plan:
    def __init__(self, grid, narrow, local_members, local_states, obs_local):
        self.nx, self.nz = grid
        self.narrow = narrow
        self.ny = narrow // 2
        self.ml = local_members
        self.m = local_members * narrow
        self.states = local_states
        self.share = local_states // narrow
        self.obs = obs_local
        self.oshare = obs_local // narrow
        self.nb = self.m // 128
        self.blocks = [(i, j) for i in range(self.nb) for j in range(i, self.nb)]
        self.half = len(self.blocks) // 2
        self.peers = self.nx * self.ny
        tiles = self.half * 8
        self.ra = tiles * 2 // 3 // self.peers * 16
        self.rb = (tiles * 16 - self.ra * self.peers) // self.nz
        self.tb = self.rb + 16
        self.base = self.ra * self.peers
        self.strip = min(256, self.m)
        assert self.half * 2 == len(self.blocks) and self.rb % 16 == 0
        assert local_members == 128 and self.base + self.rb * self.nz == self.half * 128
        self.near = sorted(((d, f) for d in range(self.ny) for f in range(2) if d + f), key=lambda k: -min(k[0], self.ny - k[0]))


def segments(plan, pos):
    out, row = [], pos * 128
    while row < (pos + 1) * 128:
        first = row < plan.base
        size = plan.ra if first else plan.rb
        piece, inside = divmod(row if first else row - plan.base, size)
        count = min(size - inside, (pos + 1) * 128 - row)
        out.append((first, piece, inside, row - pos * 128, count))
        row += count
    return out


def resplit(tail, nb):
    total = tail[:nb] + tail[nb : 2 * nb]
    high = total.astype(BF16).astype(F32)
    rest = [high, total - high]
    if 2 * nb < 16:
        rest.append(jnp.zeros((16 - 2 * nb, 128), F32))
    return jnp.concatenate(rest, axis=0)


def kernel(plan, owner, infl, oblk, ens, value, std, out, ens_v, gat, robs, scaled, part_a, part_b, core_a, core_b, chip_a,
           chip_b, xy_a, z_b, z_a, x_b, y_b, tailbuf, prow, agbuf, gram, prod, mix, est, estb, more, moreb, raw, anom, tmat, stage,
           load_sem, obs_s, obs_r, core_s, core_r, xa_s, xa_r, zb_s, zb_r, za_s, za_r, xb_s, xb_r, yb_s, yb_r, ga_s, ga_r, gb_s, gb_r,
           fa_s, fa_r, fb_s, fb_r, raw_s, raw_r, own_sem, out_s, out_r):
    p = plan
    n = lax.axis_index("narrow")
    w = lax.axis_index("wide")
    x, z = lax.div(w, p.nz), lax.rem(w, p.nz)
    y, c = lax.div(n, 2), lax.rem(n, 2)
    q0 = x * p.ny + y
    root_scale = math.sqrt(p.m - 1)
    pending = []

    def copy_to(src, dst, send, recv, device):
        return pltpu.make_async_remote_copy(
            src_ref=src, dst_ref=dst, send_sem=send, recv_sem=recv, device_id=device, device_id_type=MESH
        )

    def near(k):
        return lax.rem(y + k[0], p.ny) * 2 + (1 - c if k[1] else c)

    def along(t):
        return lax.rem(z + t, p.nz)

    def along_id(k):
        return (x * p.nz + k, n)

    def plane(t):
        return lax.rem(q0 + t, p.peers)

    def plane_id(q):
        return (lax.div(q, p.ny) * p.nz + z, lax.rem(q, p.ny) * 2 + c)

    sibling = (w, n + 1 - 2 * c)

    def each(count, step):
        def body(t, carry):
            step(t)
            return carry

        lax.fori_loop(1, count, body, 0)

    def finish(items):
        for item in items:
            if isinstance(item, tuple):
                each(item[0], lambda t: item[1](t).wait_send())
            else:
                item.wait_send()

    def load_block(b):
        cols = pl.ds(pl.multiple_of(b * 128, 128), 128)
        return pltpu.make_async_copy(ens.at[:, cols], ens_v.at[b], load_sem)

    barrier = pltpu.get_barrier_semaphore()
    greeted = 0
    for k in p.near:
        pl.semaphore_signal(barrier, inc=1, device_id=(w, near(k)), device_id_type=MESH)
        greeted += 1
    lax.fori_loop(0, p.states // 128, lambda b, carry: (load_block(b).start(), carry)[1], 0)
    for t in range(1, p.nz):
        pl.semaphore_signal(barrier, inc=1, device_id=along_id(along(t)), device_id_type=MESH)
        greeted += 1
    for dx in range(1, p.nx):
        for dy in range(p.ny):
            there = (lax.rem(x + dx, p.nx) * p.nz + z, lax.rem(y + dy, p.ny) * 2 + c)
            pl.semaphore_signal(barrier, inc=1, device_id=there, device_id_type=MESH)
            greeted += 1

    pltpu.make_async_copy(ens_v, ens_v, load_sem).wait()
    per = p.oshare // 128
    for b in range(p.obs // 128):
        gat[b // per, :, (b % per) * 128 : (b % per) * 128 + 128] = ens_v[oblk[b]]
    pl.semaphore_wait(barrier, greeted)

    def obs_copy(k):
        there = near(k)
        return copy_to(gat.at[there], robs.at[n], obs_s.at[2 * k[0] + k[1]], obs_r.at[n], (w, there))

    def obs_arrival(k):
        frm = near(k)
        return copy_to(gat.at[frm], robs.at[frm], obs_s.at[0], obs_r.at[frm], (w, frm))

    for k in p.near:
        obs_copy(k).start()
        pending.append(obs_copy(k))
    robs[pl.ds(n, 1)] = gat[pl.ds(n, 1)]
    for k in p.near:
        obs_arrival(k).wait_recv()

    def share_cols(k):
        return pl.ds(pl.multiple_of(k * p.share, 128), p.share)

    def half_cols(k, h):
        return pl.ds(pl.multiple_of(k * p.share + h * (p.share // 2), 128), p.share // 2)

    def half_slot(k, h):
        return raw.at[k, :, pl.ds(h * (p.share // 2), p.share // 2)]

    def raw_copy(k, h):
        there = near(k)
        src = ens.at[:, half_cols(there, h)]
        return copy_to(src, half_slot(n, h), raw_s.at[2 * k[0] + k[1], h], raw_r.at[n, h], (w, there))

    def raw_arrival(k, h):
        frm = near(k)
        return copy_to(ens.at[:, half_cols(frm, h)], half_slot(frm, h), raw_s.at[0, 0], raw_r.at[frm, h], (w, frm))

    def raw_start(when):
        for h in range(2):
            for k in p.near:
                if RAW_AT[min(k[0], p.ny - k[0])][2 * k[1] + h] == when:
                    raw_copy(k, h).start()
                    pending.append(raw_copy(k, h))

    own = pltpu.make_async_copy(ens.at[:, share_cols(n)], raw.at[n], own_sem.at[0])
    own.start()
    raw_start(0)

    innov = []
    for k in range(per):
        cols = slice(k * 128, k * 128 + 128)
        member = robs[:, :, cols].reshape(p.m, 128).astype(F32)
        mean = jnp.sum(member, axis=0, keepdims=True) / p.m
        ob = n * per + k
        factor = infl[owner[oblk[ob]]]
        sigma = std[pl.ds(ob, 1), :]
        shifted = (factor * (member - mean)).astype(BF16)
        scaled[:, cols] = (shifted.astype(F32) / (sigma * root_scale)).astype(BF16)
        innov.append((value[pl.ds(ob, 1), :] - mean) / sigma)
    innov = jnp.concatenate(innov, axis=1)
    high = innov.astype(BF16).astype(F32)
    middle = (innov - high).astype(BF16).astype(F32)
    low = innov - high - middle
    row_ids = lax.broadcasted_iota(jnp.int32, (16, p.oshare), 0)
    lhs = jnp.where(row_ids == 0, high, jnp.where(row_ids == 1, middle, jnp.where(row_ids == 2, low, 0.0)))
    projected = lax.dot_general(lhs.astype(BF16), scaled[...], NT, preferred_element_type=F32)
    projected = jnp.sum(projected, axis=0, keepdims=True)
    tailbuf[...] = jnp.zeros_like(tailbuf)
    for i in range(p.nb):
        tailbuf[i : i + 1, :] = projected[:, i * 128 : i * 128 + 128]
    tail = resplit(tailbuf[...], p.nb).astype(BF16)
    for h in range(2):
        part_b[h, 0, p.rb :, :] = tail
        for k in range(1, p.nz):
            part_b[h, k, p.rb :, :] = jnp.zeros_like(tail)
    index = 0
    for i in range(p.nb):
        rows = lax.dot_general(
            scaled[i * 128 : i * 128 + 128, :], scaled[i * 128 :, :], NT, preferred_element_type=F32
        ).astype(BF16)
        for j in range(i, p.nb):
            h, pos = divmod(index, p.half)
            for first, piece, inside, start, count in segments(p, pos):
                ref = part_a if first else part_b
                ref[h, piece, inside : inside + count, :] = rows[start : start + count, (j - i) * 128 : (j - i) * 128 + 128]
            index += 1

    core_copy_b = copy_to(part_b.at[1 - c], core_b, core_s.at[0], core_r.at[0], sibling)
    core_copy_a = copy_to(part_a.at[1 - c], core_a, core_s.at[1], core_r.at[1], sibling)
    core_copy_b.start()
    core_copy_a.start()
    pending += [core_copy_a, core_copy_b]

    def zb_copy(t):
        there = along(t)
        return copy_to(chip_b.at[there], z_b.at[z], zb_s.at[t], zb_r.at[z], along_id(there))

    def zb_arrival(t):
        frm = along(t)
        return copy_to(chip_b.at[frm], z_b.at[frm], zb_s.at[0], zb_r.at[frm], along_id(frm))

    def xa_copy(t):
        there = plane(t)
        return copy_to(chip_a.at[there], xy_a.at[q0], xa_s.at[t], xa_r.at[q0], plane_id(there))

    def xa_arrival(t):
        frm = plane(t)
        return copy_to(chip_a.at[frm], xy_a.at[frm], xa_s.at[0], xa_r.at[frm], plane_id(frm))

    def add_b(k, carry):
        total = part_b[c, k, : p.rb, :].astype(F32) + core_b[k, : p.rb, :].astype(F32)
        chip_b[k, : p.rb, :] = total.astype(BF16)
        chip_b[k, p.rb :, :] = tail
        return carry

    def add_a(k, carry):
        chip_a[k] = (part_a[c, k].astype(F32) + core_a[k].astype(F32)).astype(BF16)
        return carry

    core_copy_b.wait_recv()
    tail = resplit(part_b[c, 0, p.rb :, :].astype(F32) + core_b[0, p.rb :, :].astype(F32), p.nb).astype(BF16)
    lax.fori_loop(0, p.nz, add_b, 0)
    each(p.nz, lambda t: zb_copy(t).start())
    core_copy_a.wait_recv()
    lax.fori_loop(0, p.peers, add_a, 0)
    each(p.peers, lambda t: xa_copy(t).start())
    pending += [(p.nz, zb_copy), (p.peers, xa_copy)]
    raw_start(1)

    def za_copy(t):
        return copy_to(z_a.at[z], z_a.at[z], za_s.at[t], za_r.at[z], along_id(along(t)))

    def za_arrival(t):
        frm = along(t)
        return copy_to(z_a.at[frm], z_a.at[frm], za_s.at[0], za_r.at[frm], along_id(frm))

    def x_id(t):
        return (lax.rem(x + t, p.nx) * p.nz + z, n)

    def y_id(t):
        return (w, lax.rem(y + t, p.ny) * 2 + c)

    def xb_copy(t):
        return copy_to(x_b.at[x], x_b.at[x], xb_s.at[t], xb_r.at[x], x_id(t))

    def xb_arrival(t):
        frm = lax.rem(x + t, p.nx)
        return copy_to(x_b.at[frm], x_b.at[frm], xb_s.at[0], xb_r.at[frm], x_id(t))

    def yb_copy(t):
        return copy_to(y_b.at[y], y_b.at[y], yb_s.at[t], yb_r.at[y], y_id(t))

    def yb_arrival(t):
        frm = lax.rem(y + t, p.ny)
        return copy_to(y_b.at[frm], y_b.at[frm], yb_s.at[0], yb_r.at[frm], y_id(t))

    def take(arrival, ref, turn):
        def body(t, total):
            arrival(t).wait_recv()
            return total + ref[turn(t)].astype(F32)

        return body

    def put_b(ref, at, total):
        ref[at, : p.rb, :] = total[: p.rb].astype(BF16)
        ref[at, p.rb :, :] = resplit(total[p.rb :], p.nb).astype(BF16)

    put_b(x_b, x, lax.fori_loop(1, p.nz, take(zb_arrival, z_b, along), chip_b[z].astype(F32)))
    each(p.nx, lambda t: xb_copy(t).start())
    total = lax.fori_loop(1, p.peers, take(xa_arrival, xy_a, plane), chip_a[q0].astype(F32))
    z_a[z] = total.astype(BF16)
    each(p.nz, lambda t: za_copy(t).start())
    put_b(y_b, y, lax.fori_loop(1, p.nx, take(xb_arrival, x_b, lambda t: lax.rem(x + t, p.nx)), x_b[x].astype(F32)))
    each(p.ny, lambda t: yb_copy(t).start())
    pending += [(p.nx, xb_copy), (p.nz, za_copy), (p.ny, yb_copy)]
    raw_start(2)

    def rows_a(q):
        return pl.ds(pl.multiple_of(q * p.ra, 16), p.ra)

    def rows_b(k):
        return pl.ds(pl.multiple_of(p.base + k * p.rb, 16), p.rb)

    def ga_copy(t):
        mine = agbuf.at[c, rows_a(q0), :]
        return copy_to(mine, mine, ga_s.at[t], ga_r.at[q0], plane_id(plane(t)))

    def ga_arrival(t):
        slot = agbuf.at[c, rows_a(plane(t)), :]
        return copy_to(slot, slot, ga_s.at[0], ga_r.at[plane(t)], plane_id(plane(t)))

    def gb_copy(t):
        mine = agbuf.at[c, rows_b(z), :]
        return copy_to(mine, mine, gb_s.at[t], gb_r.at[z], along_id(along(t)))

    def gb_arrival(t):
        slot = agbuf.at[c, rows_b(along(t)), :]
        return copy_to(slot, slot, gb_s.at[0], gb_r.at[along(t)], along_id(along(t)))

    def fa_copy(t):
        slot = agbuf.at[c, rows_a(plane(t)), :]
        return copy_to(slot, slot, fa_s.at[t], fa_r.at[plane(t)], sibling)

    def fb_copy(t):
        slot = agbuf.at[c, rows_b(along(t)), :]
        return copy_to(slot, slot, fb_s.at[t], fb_r.at[along(t)], sibling)

    def fa_arrival(q):
        slot = agbuf.at[1 - c, rows_a(q), :]
        return copy_to(slot, slot, fa_s.at[0], fa_r.at[q], sibling)

    def fb_arrival(k):
        slot = agbuf.at[1 - c, rows_b(k), :]
        return copy_to(slot, slot, fb_s.at[0], fb_r.at[k], sibling)

    total = lax.fori_loop(1, p.nz, take(za_arrival, z_a, along), z_a[z].astype(F32))
    agbuf[c, rows_a(q0), :] = total.astype(BF16)
    each(p.peers, lambda t: ga_copy(t).start())
    fa_copy(0).start()
    total = lax.fori_loop(1, p.ny, take(yb_arrival, y_b, lambda t: lax.rem(y + t, p.ny)), y_b[y].astype(F32))
    agbuf[c, rows_b(z), :] = total[: p.rb].astype(BF16)
    each(p.nz, lambda t: gb_copy(t).start())
    fb_copy(0).start()
    pending += [(p.peers, ga_copy), (p.nz, gb_copy), (p.peers, fa_copy), (p.nz, fb_copy), fa_copy(0), fb_copy(0)]
    raw_start(3)
    for i in range(p.nb):
        row = total[p.rb + i : p.rb + i + 1] + total[p.rb + p.nb + i : p.rb + p.nb + i + 1]
        prow[:, i * 128 : i * 128 + 128] = row

    def pass_a(t):
        ga_arrival(t).wait_recv()
        fa_copy(t).start()

    def pass_b(t):
        gb_arrival(t).wait_recv()
        fb_copy(t).start()

    each(p.nz, pass_b)
    each(p.peers, pass_a)
    raw_start(4)
    lax.fori_loop(0, p.nz, lambda k, carry: (fb_arrival(k).wait_recv(), carry)[1], 0)
    lax.fori_loop(0, p.peers, lambda q, carry: (fa_arrival(q).wait_recv(), carry)[1], 0)

    diag = lax.broadcasted_iota(jnp.int32, (128, 128), 0) == lax.broadcasted_iota(jnp.int32, (128, 128), 1)
    eye = diag.astype(F32)
    square = jnp.zeros((128, 128), F32)
    index = 0
    for i in range(p.nb):
        for j in range(i, p.nb):
            h, pos = divmod(index, p.half)
            block = agbuf[h, pos * 128 : pos * 128 + 128, :]
            wide = block.astype(F32)
            if i == j:
                wide = wide + eye
                block = wide.astype(BF16)
                square = square + wide * wide
            else:
                square = square + 2.0 * (wide * wide)
                gram[j * 128 : j * 128 + 128, i * 128 : i * 128 + 128] = wide.T.astype(BF16)
            gram[i * 128 : i * 128 + 128, j * 128 : j * 128 + 128] = block
            index += 1
    square = jnp.sum(jnp.sum(square, axis=0, keepdims=True), axis=1, keepdims=True)
    frob = jnp.sqrt(square)
    inv = 1.0 / frob

    strips = p.m // p.strip

    def mm(a, b):
        return jnp.dot(a, b, preferred_element_type=F32)

    def put(ref, s, value):
        cols = slice(s * p.strip, (s + 1) * p.strip)
        value = value.astype(ref.dtype)
        ref[: (s + 1) * p.strip, cols] = value
        if s > 0:
            ref[cols, : s * p.strip] = value[: s * p.strip].T

    def corner(s):
        return slice(0, (s + 1) * p.strip), slice(s * p.strip, (s + 1) * p.strip)

    for s in reversed(range(strips)):
        rows, cols = corner(s)
        unit = gram[rows, cols].astype(F32) * inv
        unit2 = mm(gram[rows, :], gram[:, cols]) * (inv * inv)
        put(prod, s, unit2)
        put(mix, s, 0.0625 * unit2 - 0.5625 * unit)
        est[rows, cols] = 1.6875 * unit2 - 2.4375 * unit
    for s in reversed(range(strips)):
        rows, cols = corner(s)
        new = est[rows, cols] + mm(prod[rows, :], mix[:, cols])
        est[rows, cols] = new
        put(estb, s, new)
    for s in reversed(range(strips)):
        rows, cols = corner(s)
        half = gram[rows, cols].astype(F32) * (2.25 * inv) + mm(gram[rows, :], estb[:, cols]) * inv
        more[rows, cols] = half
        put(prod, s, half)
    for s in reversed(range(strips)):
        rows, cols = corner(s)
        unit = 2.25 * more[rows, cols] + mm(prod[rows, :], estb[:, cols])
        more[rows, cols] = unit
        put(mix, s, unit)
    for s in reversed(range(strips)):
        rows, cols = corner(s)
        unit = more[rows, cols]
        unit2 = mm(mix[rows, :], mix[:, cols])
        put(prod, s, unit2)
        put(moreb, s, 0.0625 * unit2 - 0.5625 * unit)
        more[rows, cols] = 1.6875 * unit2 - 2.4375 * unit
    for s in reversed(range(strips)):
        rows, cols = corner(s)
        new = more[rows, cols] + mm(prod[rows, :], moreb[:, cols])
        put(mix, s, new)
        est[rows, cols] = 2.25 * (est[rows, cols] + new)
    for s in reversed(range(strips)):
        rows, cols = corner(s)
        new = est[rows, cols] + mm(estb[rows, :], mix[:, cols])
        row_ids = lax.broadcasted_iota(jnp.int32, new.shape, 0)
        col_ids = lax.broadcasted_iota(jnp.int32, new.shape, 1) + s * p.strip
        put(est, s, new + jnp.where(row_ids == col_ids, 2.25 * 2.25, 0.0))

    inv_root = lax.rsqrt(frob)

    def shift_rows(s, total):
        rows = pl.ds(pl.multiple_of(s * 128, 128), 128)
        block = est[rows, :]
        midway = jnp.sum(block * prow[...], axis=1, keepdims=True)
        return total + jnp.sum(block * midway, axis=0, keepdims=True)

    shift = lax.fori_loop(0, p.m // 128, shift_rows, jnp.zeros((1, p.m), F32))
    shift = shift * (inv / root_scale)

    def transform_rows(s, carry):
        rows = pl.ds(pl.multiple_of(s * 128, 128), 128)
        tmat[rows, :] = (est[rows, :] * inv_root + shift).astype(BF16)
        return carry

    lax.fori_loop(0, p.m // 128, transform_rows, 0)

    per_half = p.share // 2

    def out_copy(dy, core, h):
        there = lax.rem(y + dy, p.ny) * 2 + core
        cols = pl.ds(h * per_half, per_half)
        return copy_to(
            stage.at[dy, pl.ds(core * 128, 128), cols], out.at[:, half_cols(n, h)], out_s.at[dy, core, h], out_r.at[n, h], (w, there)
        )

    def out_arrival(k, h):
        cols = pl.ds(h * per_half, per_half)
        slot = out.at[:, half_cols(near(k), h)]
        return copy_to(stage.at[0, pl.ds(0, 128), cols], slot, out_s.at[0, 0, h], out_r.at[near(k), h], (w, near(k)))

    def analyse(dy, h, mean):
        rows = pl.ds(pl.multiple_of(lax.rem(y + dy, p.ny) * 256, 256), 256)
        cols = slice(h * per_half, (h + 1) * per_half)
        stage[dy, :, cols] = (mean + mm(tmat[rows, :], anom[:, cols])).astype(BF16)

    order = sorted(range(1, p.ny), key=lambda d: -min(d, p.ny - d))
    means = []
    early, pending = pending, []
    for h in range(2):
        for k in p.near:
            raw_arrival(k, h).wait_recv()
        if h == 0:
            own.wait()
        cols = slice(h * per_half, (h + 1) * per_half)
        mean = jnp.zeros((1, per_half), F32)
        for k in range(p.narrow):
            mean = mean + jnp.sum(raw[k, :, cols].astype(F32), axis=0, keepdims=True)
        mean = mean / p.m
        means.append(mean)
        first = n * (p.share // 128) + h * (per_half // 128)
        factors = [jnp.full((1, 128), infl[owner[first + b]], F32) for b in range(per_half // 128)]
        factors = jnp.concatenate(factors, axis=1)
        for k in range(p.narrow):
            anom[k * 128 : k * 128 + 128, cols] = (factors * (raw[k, :, cols].astype(F32) - mean)).astype(BF16)
        for dy in order:
            analyse(dy, h, mean)
            for core in range(2):
                out_copy(dy, core, h).start()
                pending.append(out_copy(dy, core, h))
    for h in range(2):
        analyse(0, h, means[h])
    rest = []
    for h in range(2):
        cols = pl.ds(h * per_half, per_half)
        theirs = stage.at[0, pl.ds(pl.multiple_of((1 - c) * 128, 128), 128), cols]
        mine = stage.at[0, pl.ds(pl.multiple_of(c * 128, 128), 128), cols]
        to_sibling = copy_to(theirs, out.at[:, half_cols(n, h)], out_s.at[0, 0, h], out_r.at[n, h], sibling)
        to_sibling.start()
        pending.append(to_sibling)
        keep = pltpu.make_async_copy(mine, out.at[:, half_cols(n, h)], own_sem.at[h])
        keep.start()
        rest.append(keep)
    finish(early)
    for keep in rest:
        keep.wait()
    for h in range(2):
        for k in reversed(p.near):
            out_arrival(k, h).wait_recv()
    finish(pending)


def hand_on(parts, done, out, hold, in_sems, out_sems):
    rows = [pl.ds(k * (done.shape[0] // parts), done.shape[0] // parts) for k in range(parts)]
    reads = [pltpu.make_async_copy(done.at[r], hold.at[r], in_sems.at[k]) for k, r in enumerate(rows)]
    writes = [pltpu.make_async_copy(hold.at[r], out.at[r], out_sems.at[k]) for k, r in enumerate(rows)]
    for read in reads:
        read.start()
    for read, write in zip(reads, writes):
        read.wait()
        write.start()
    for write in writes:
        write.wait()


def on_device(grid, narrow, ensemble, owner, inflation, obs_block, obs_value, obs_std):
    p = Plan(grid, narrow, *ensemble.shape, obs_value.shape[0])
    dma = pltpu.SemaphoreType.DMA
    vmem, smem = pl.BlockSpec(memory_space=pltpu.VMEM), pl.BlockSpec(memory_space=pltpu.SMEM)
    anywhere = pl.BlockSpec(memory_space=pl.ANY)
    square = (p.m, p.m)
    scratch = [
        pltpu.VMEM((p.states // 128, p.ml, 128), BF16),
        pltpu.VMEM((p.narrow, p.ml, p.oshare), BF16),
        pltpu.VMEM((p.narrow, p.ml, p.oshare), BF16),
        pltpu.VMEM((p.m, p.oshare), BF16),
        pltpu.VMEM((2, p.peers, p.ra, 128), BF16),
        pltpu.VMEM((2, p.nz, p.tb, 128), BF16),
        pltpu.VMEM((p.peers, p.ra, 128), BF16),
        pltpu.VMEM((p.nz, p.tb, 128), BF16),
        pltpu.VMEM((p.peers, p.ra, 128), BF16),
        pltpu.VMEM((p.nz, p.tb, 128), BF16),
        pltpu.VMEM((p.peers, p.ra, 128), BF16),
        pltpu.VMEM((p.nz, p.tb, 128), BF16),
        pltpu.VMEM((p.nz, p.ra, 128), BF16),
        pltpu.VMEM((p.nx, p.tb, 128), BF16),
        pltpu.VMEM((p.ny, p.tb, 128), BF16),
        pltpu.VMEM((16, 128), F32),
        pltpu.VMEM((1, p.m), F32),
        pltpu.VMEM((2, p.half * 128, 128), BF16),
        pltpu.VMEM(square, BF16),
        pltpu.VMEM(square, BF16),
        pltpu.VMEM(square, BF16),
        pltpu.VMEM(square, F32),
        pltpu.VMEM(square, BF16),
        pltpu.VMEM(square, F32),
        pltpu.VMEM(square, BF16),
        pltpu.VMEM((p.narrow, p.ml, p.share), BF16),
        pltpu.VMEM((p.m, p.share), BF16),
        pltpu.VMEM(square, BF16),
        pltpu.VMEM((p.ny, 256, p.share), BF16),
        dma, dma((p.narrow,)), dma((p.narrow,)),
        dma((2,)), dma((2,)),
        dma((p.peers,)), dma((p.peers,)), dma((p.nz,)), dma((p.nz,)),
        dma((p.nz,)), dma((p.nz,)), dma((p.nx,)), dma((p.nx,)), dma((p.ny,)), dma((p.ny,)),
        dma((p.peers,)), dma((p.peers,)), dma((p.nz,)), dma((p.nz,)),
        dma((p.peers,)), dma((p.peers,)), dma((p.nz,)), dma((p.nz,)),
        dma((p.narrow, 2)), dma((p.narrow, 2)),
        dma((2,)), dma((p.ny, 2, 2)), dma((p.narrow, 2)),
    ]
    done = pl.pallas_call(
        functools.partial(kernel, p),
        out_shape=jax.ShapeDtypeStruct(ensemble.shape, BF16),
        in_specs=[smem, smem, smem, anywhere, vmem, vmem],
        out_specs=anywhere,
        scratch_shapes=scratch,
        compiler_params=pltpu.CompilerParams(
            collective_id=0, has_side_effects=True, vmem_limit_bytes=56 * 1024 * 1024
        ),
        name="etkf",
    )(owner, inflation, obs_block, ensemble, obs_value.reshape(-1, 128), obs_std.reshape(-1, 128))
    parts = p.ml // 16
    return pl.pallas_call(
        functools.partial(hand_on, parts),
        out_shape=jax.ShapeDtypeStruct(ensemble.shape, BF16),
        in_specs=[anywhere],
        out_specs=anywhere,
        scratch_shapes=[pltpu.VMEM(ensemble.shape, BF16), dma((parts,)), dma((parts,))],
        compiler_params=pltpu.CompilerParams(vmem_limit_bytes=56 * 1024 * 1024),
        name="hand_on",
    )(done)


def solution(mesh):
    wide, narrow = mesh.shape["wide"], mesh.shape["narrow"]
    grid = (4, wide // 4) if wide >= 16 else (2, wide // 2)
    return jax.shard_map(
        functools.partial(on_device, grid, narrow),
        mesh=mesh,
        in_specs=(P("narrow", "wide"), P("wide"), P(), P("wide"), P("wide"), P("wide")),
        out_specs=P("narrow", "wide"),
        check_vma=False,
    )
```

```python
import functools
import math

import jax
import jax.numpy as jnp
from jax import lax
from jax.experimental import pallas as pl
from jax.experimental.pallas import tpu as pltpu
from jax.sharding import PartitionSpec as P

CLASSES = 128
MESH = pl.DeviceIdType.MESH
F32 = jnp.float32
BF16 = jnp.bfloat16
NT = (((1,), (1,)), ((), ()))
RAW_AT = ((None, None, 0, 0), (4, 4, 4, 4), (0, 2, 1, 4))


class Plan:
    def __init__(self, grid, narrow, local_members, local_states, obs_local):
        self.nx, self.nz = grid
        self.narrow = narrow
        self.ny = narrow // 2
        self.ml = local_members
        self.m = local_members * narrow
        self.states = local_states
        self.share = local_states // narrow
        self.obs = obs_local
        self.oshare = obs_local // narrow
        self.nb = self.m // 128
        self.blocks = [(i, j) for i in range(self.nb) for j in range(i, self.nb)]
        self.half = len(self.blocks) // 2
        self.peers = self.nx * self.ny
        tiles = self.half * 8
        self.ra = tiles * 2 // 3 // self.peers * 16
        self.rb = (tiles * 16 - self.ra * self.peers) // self.nz
        self.tb = self.rb + 16
        self.base = self.ra * self.peers
        self.strip = min(256, self.m)
        assert self.half * 2 == len(self.blocks) and self.rb % 16 == 0
        assert local_members == 128 and self.base + self.rb * self.nz == self.half * 128
        self.near = sorted(((d, f) for d in range(self.ny) for f in range(2) if d + f), key=lambda k: -min(k[0], self.ny - k[0]))


def segments(plan, pos):
    out, row = [], pos * 128
    while row < (pos + 1) * 128:
        first = row < plan.base
        size = plan.ra if first else plan.rb
        piece, inside = divmod(row if first else row - plan.base, size)
        count = min(size - inside, (pos + 1) * 128 - row)
        out.append((first, piece, inside, row - pos * 128, count))
        row += count
    return out


def resplit(tail, nb):
    total = tail[:nb] + tail[nb : 2 * nb]
    high = total.astype(BF16).astype(F32)
    rest = [high, total - high]
    if 2 * nb < 16:
        rest.append(jnp.zeros((16 - 2 * nb, 128), F32))
    return jnp.concatenate(rest, axis=0)


def kernel(plan, owner, infl, oblk, ens, value, std, out, ens_v, gat, robs, scaled, part_a, part_b, core_a, core_b, chip_a,
           chip_b, xy_a, z_b, z_a, x_b, y_b, tailbuf, prow, agbuf, gram, prod, mix, est, estb, more, moreb, raw, anom, tmat, stage,
           load_sem, obs_s, obs_r, core_s, core_r, xa_s, xa_r, zb_s, zb_r, za_s, za_r, xb_s, xb_r, yb_s, yb_r, ga_s, ga_r, gb_s, gb_r,
           fa_s, fa_r, fb_s, fb_r, raw_s, raw_r, own_sem, out_s, out_r):
    p = plan
    n = lax.axis_index("narrow")
    w = lax.axis_index("wide")
    x, z = lax.div(w, p.nz), lax.rem(w, p.nz)
    y, c = lax.div(n, 2), lax.rem(n, 2)
    q0 = x * p.ny + y
    root_scale = math.sqrt(p.m - 1)
    pending = []

    def copy_to(src, dst, send, recv, device):
        return pltpu.make_async_remote_copy(
            src_ref=src, dst_ref=dst, send_sem=send, recv_sem=recv, device_id=device, device_id_type=MESH
        )

    def near(k):
        return lax.rem(y + k[0], p.ny) * 2 + (1 - c if k[1] else c)

    def along(t):
        return lax.rem(z + t, p.nz)

    def along_id(k):
        return (x * p.nz + k, n)

    def plane(t):
        return lax.rem(q0 + t, p.peers)

    def plane_id(q):
        return (lax.div(q, p.ny) * p.nz + z, lax.rem(q, p.ny) * 2 + c)

    sibling = (w, n + 1 - 2 * c)

    def each(count, step):
        def body(t, carry):
            step(t)
            return carry

        lax.fori_loop(1, count, body, 0)

    def finish(items):
        for item in items:
            if isinstance(item, tuple):
                each(item[0], lambda t: item[1](t).wait_send())
            else:
                item.wait_send()

    def load_block(b):
        cols = pl.ds(pl.multiple_of(b * 128, 128), 128)
        return pltpu.make_async_copy(ens.at[:, cols], ens_v.at[b], load_sem)

    barrier = pltpu.get_barrier_semaphore()
    greeted = 0
    for k in p.near:
        pl.semaphore_signal(barrier, inc=1, device_id=(w, near(k)), device_id_type=MESH)
        greeted += 1
    lax.fori_loop(0, p.states // 128, lambda b, carry: (load_block(b).start(), carry)[1], 0)
    for t in range(1, p.nz):
        pl.semaphore_signal(barrier, inc=1, device_id=along_id(along(t)), device_id_type=MESH)
        greeted += 1
    for dx in range(1, p.nx):
        for dy in range(p.ny):
            there = (lax.rem(x + dx, p.nx) * p.nz + z, lax.rem(y + dy, p.ny) * 2 + c)
            pl.semaphore_signal(barrier, inc=1, device_id=there, device_id_type=MESH)
            greeted += 1

    pltpu.make_async_copy(ens_v, ens_v, load_sem).wait()
    per = p.oshare // 128
    for b in range(p.obs // 128):
        gat[b // per, :, (b % per) * 128 : (b % per) * 128 + 128] = ens_v[oblk[b]]
    pl.semaphore_wait(barrier, greeted)

    def obs_copy(k):
        there = near(k)
        return copy_to(gat.at[there], robs.at[n], obs_s.at[2 * k[0] + k[1]], obs_r.at[n], (w, there))

    def obs_arrival(k):
        frm = near(k)
        return copy_to(gat.at[frm], robs.at[frm], obs_s.at[0], obs_r.at[frm], (w, frm))

    for k in p.near:
        obs_copy(k).start()
        pending.append(obs_copy(k))
    robs[pl.ds(n, 1)] = gat[pl.ds(n, 1)]
    for k in p.near:
        obs_arrival(k).wait_recv()

    def share_cols(k):
        return pl.ds(pl.multiple_of(k * p.share, 128), p.share)

    def half_cols(k, h):
        return pl.ds(pl.multiple_of(k * p.share + h * (p.share // 2), 128), p.share // 2)

    def half_slot(k, h):
        return raw.at[k, :, pl.ds(h * (p.share // 2), p.share // 2)]

    def raw_copy(k, h):
        there = near(k)
        src = ens.at[:, half_cols(there, h)]
        return copy_to(src, half_slot(n, h), raw_s.at[2 * k[0] + k[1], h], raw_r.at[n, h], (w, there))

    def raw_arrival(k, h):
        frm = near(k)
        return copy_to(ens.at[:, half_cols(frm, h)], half_slot(frm, h), raw_s.at[0, 0], raw_r.at[frm, h], (w, frm))

    def raw_start(when):
        for h in range(2):
            for k in p.near:
                if RAW_AT[min(k[0], p.ny - k[0])][2 * k[1] + h] == when:
                    raw_copy(k, h).start()
                    pending.append(raw_copy(k, h))

    own = pltpu.make_async_copy(ens.at[:, share_cols(n)], raw.at[n], own_sem.at[0])
    own.start()
    raw_start(0)

    innov = []
    for k in range(per):
        cols = slice(k * 128, k * 128 + 128)
        member = robs[:, :, cols].reshape(p.m, 128).astype(F32)
        mean = jnp.sum(member, axis=0, keepdims=True) / p.m
        ob = n * per + k
        factor = infl[owner[oblk[ob]]]
        sigma = std[pl.ds(ob, 1), :]
        shifted = (factor * (member - mean)).astype(BF16)
        scaled[:, cols] = (shifted.astype(F32) / (sigma * root_scale)).astype(BF16)
        innov.append((value[pl.ds(ob, 1), :] - mean) / sigma)
    innov = jnp.concatenate(innov, axis=1)
    high = innov.astype(BF16).astype(F32)
    middle = (innov - high).astype(BF16).astype(F32)
    low = innov - high - middle
    row_ids = lax.broadcasted_iota(jnp.int32, (16, p.oshare), 0)
    lhs = jnp.where(row_ids == 0, high, jnp.where(row_ids == 1, middle, jnp.where(row_ids == 2, low, 0.0)))
    projected = lax.dot_general(lhs.astype(BF16), scaled[...], NT, preferred_element_type=F32)
    projected = jnp.sum(projected, axis=0, keepdims=True)
    tailbuf[...] = jnp.zeros_like(tailbuf)
    for i in range(p.nb):
        tailbuf[i : i + 1, :] = projected[:, i * 128 : i * 128 + 128]
    tail = resplit(tailbuf[...], p.nb).astype(BF16)
    for h in range(2):
        part_b[h, 0, p.rb :, :] = tail
        for k in range(1, p.nz):
            part_b[h, k, p.rb :, :] = jnp.zeros_like(tail)
    index = 0
    for i in range(p.nb):
        rows = lax.dot_general(
            scaled[i * 128 : i * 128 + 128, :], scaled[i * 128 :, :], NT, preferred_element_type=F32
        ).astype(BF16)
        for j in range(i, p.nb):
            h, pos = divmod(index, p.half)
            for first, piece, inside, start, count in segments(p, pos):
                ref = part_a if first else part_b
                ref[h, piece, inside : inside + count, :] = rows[start : start + count, (j - i) * 128 : (j - i) * 128 + 128]
            index += 1

    core_copy_b = copy_to(part_b.at[1 - c], core_b, core_s.at[0], core_r.at[0], sibling)
    core_copy_a = copy_to(part_a.at[1 - c], core_a, core_s.at[1], core_r.at[1], sibling)
    core_copy_b.start()
    core_copy_a.start()
    pending += [core_copy_a, core_copy_b]

    def zb_copy(t):
        there = along(t)
        return copy_to(chip_b.at[there], z_b.at[z], zb_s.at[t], zb_r.at[z], along_id(there))

    def zb_arrival(t):
        frm = along(t)
        return copy_to(chip_b.at[frm], z_b.at[frm], zb_s.at[0], zb_r.at[frm], along_id(frm))

    def xa_copy(t):
        there = plane(t)
        return copy_to(chip_a.at[there], xy_a.at[q0], xa_s.at[t], xa_r.at[q0], plane_id(there))

    def xa_arrival(t):
        frm = plane(t)
        return copy_to(chip_a.at[frm], xy_a.at[frm], xa_s.at[0], xa_r.at[frm], plane_id(frm))

    def add_b(k, carry):
        total = part_b[c, k, : p.rb, :].astype(F32) + core_b[k, : p.rb, :].astype(F32)
        chip_b[k, : p.rb, :] = total.astype(BF16)
        chip_b[k, p.rb :, :] = tail
        return carry

    def add_a(k, carry):
        chip_a[k] = (part_a[c, k].astype(F32) + core_a[k].astype(F32)).astype(BF16)
        return carry

    core_copy_b.wait_recv()
    tail = resplit(part_b[c, 0, p.rb :, :].astype(F32) + core_b[0, p.rb :, :].astype(F32), p.nb).astype(BF16)
    lax.fori_loop(0, p.nz, add_b, 0)
    each(p.nz, lambda t: zb_copy(t).start())
    core_copy_a.wait_recv()
    lax.fori_loop(0, p.peers, add_a, 0)
    each(p.peers, lambda t: xa_copy(t).start())
    pending += [(p.nz, zb_copy), (p.peers, xa_copy)]
    raw_start(1)

    def za_copy(t):
        return copy_to(z_a.at[z], z_a.at[z], za_s.at[t], za_r.at[z], along_id(along(t)))

    def za_arrival(t):
        frm = along(t)
        return copy_to(z_a.at[frm], z_a.at[frm], za_s.at[0], za_r.at[frm], along_id(frm))

    def x_id(t):
        return (lax.rem(x + t, p.nx) * p.nz + z, n)

    def y_id(t):
        return (w, lax.rem(y + t, p.ny) * 2 + c)

    def xb_copy(t):
        return copy_to(x_b.at[x], x_b.at[x], xb_s.at[t], xb_r.at[x], x_id(t))

    def xb_arrival(t):
        frm = lax.rem(x + t, p.nx)
        return copy_to(x_b.at[frm], x_b.at[frm], xb_s.at[0], xb_r.at[frm], x_id(t))

    def yb_copy(t):
        return copy_to(y_b.at[y], y_b.at[y], yb_s.at[t], yb_r.at[y], y_id(t))

    def yb_arrival(t):
        frm = lax.rem(y + t, p.ny)
        return copy_to(y_b.at[frm], y_b.at[frm], yb_s.at[0], yb_r.at[frm], y_id(t))

    def take(arrival, ref, turn):
        def body(t, total):
            arrival(t).wait_recv()
            return total + ref[turn(t)].astype(F32)

        return body

    def put_b(ref, at, total):
        ref[at, : p.rb, :] = total[: p.rb].astype(BF16)
        ref[at, p.rb :, :] = resplit(total[p.rb :], p.nb).astype(BF16)

    put_b(x_b, x, lax.fori_loop(1, p.nz, take(zb_arrival, z_b, along), chip_b[z].astype(F32)))
    each(p.nx, lambda t: xb_copy(t).start())
    total = lax.fori_loop(1, p.peers, take(xa_arrival, xy_a, plane), chip_a[q0].astype(F32))
    z_a[z] = total.astype(BF16)
    each(p.nz, lambda t: za_copy(t).start())
    put_b(y_b, y, lax.fori_loop(1, p.nx, take(xb_arrival, x_b, lambda t: lax.rem(x + t, p.nx)), x_b[x].astype(F32)))
    each(p.ny, lambda t: yb_copy(t).start())
    pending += [(p.nx, xb_copy), (p.nz, za_copy), (p.ny, yb_copy)]
    raw_start(2)

    def rows_a(q):
        return pl.ds(pl.multiple_of(q * p.ra, 16), p.ra)

    def rows_b(k):
        return pl.ds(pl.multiple_of(p.base + k * p.rb, 16), p.rb)

    def ga_copy(t):
        mine = agbuf.at[c, rows_a(q0), :]
        return copy_to(mine, mine, ga_s.at[t], ga_r.at[q0], plane_id(plane(t)))

    def ga_arrival(t):
        slot = agbuf.at[c, rows_a(plane(t)), :]
        return copy_to(slot, slot, ga_s.at[0], ga_r.at[plane(t)], plane_id(plane(t)))

    def gb_copy(t):
        mine = agbuf.at[c, rows_b(z), :]
        return copy_to(mine, mine, gb_s.at[t], gb_r.at[z], along_id(along(t)))

    def gb_arrival(t):
        slot = agbuf.at[c, rows_b(along(t)), :]
        return copy_to(slot, slot, gb_s.at[0], gb_r.at[along(t)], along_id(along(t)))

    def fa_copy(t):
        slot = agbuf.at[c, rows_a(plane(t)), :]
        return copy_to(slot, slot, fa_s.at[t], fa_r.at[plane(t)], sibling)

    def fb_copy(t):
        slot = agbuf.at[c, rows_b(along(t)), :]
        return copy_to(slot, slot, fb_s.at[t], fb_r.at[along(t)], sibling)

    def fa_arrival(q):
        slot = agbuf.at[1 - c, rows_a(q), :]
        return copy_to(slot, slot, fa_s.at[0], fa_r.at[q], sibling)

    def fb_arrival(k):
        slot = agbuf.at[1 - c, rows_b(k), :]
        return copy_to(slot, slot, fb_s.at[0], fb_r.at[k], sibling)

    total = lax.fori_loop(1, p.nz, take(za_arrival, z_a, along), z_a[z].astype(F32))
    agbuf[c, rows_a(q0), :] = total.astype(BF16)
    each(p.peers, lambda t: ga_copy(t).start())
    fa_copy(0).start()
    total = lax.fori_loop(1, p.ny, take(yb_arrival, y_b, lambda t: lax.rem(y + t, p.ny)), y_b[y].astype(F32))
    agbuf[c, rows_b(z), :] = total[: p.rb].astype(BF16)
    each(p.nz, lambda t: gb_copy(t).start())
    fb_copy(0).start()
    pending += [(p.peers, ga_copy), (p.nz, gb_copy), (p.peers, fa_copy), (p.nz, fb_copy), fa_copy(0), fb_copy(0)]
    raw_start(3)
    for i in range(p.nb):
        row = total[p.rb + i : p.rb + i + 1] + total[p.rb + p.nb + i : p.rb + p.nb + i + 1]
        prow[:, i * 128 : i * 128 + 128] = row

    def pass_a(t):
        ga_arrival(t).wait_recv()
        fa_copy(t).start()

    def pass_b(t):
        gb_arrival(t).wait_recv()
        fb_copy(t).start()

    each(p.nz, pass_b)
    each(p.peers, pass_a)
    raw_start(4)
    lax.fori_loop(0, p.nz, lambda k, carry: (fb_arrival(k).wait_recv(), carry)[1], 0)
    lax.fori_loop(0, p.peers, lambda q, carry: (fa_arrival(q).wait_recv(), carry)[1], 0)

    diag = lax.broadcasted_iota(jnp.int32, (128, 128), 0) == lax.broadcasted_iota(jnp.int32, (128, 128), 1)
    eye = diag.astype(F32)
    square = jnp.zeros((128, 128), F32)
    index = 0
    for i in range(p.nb):
        for j in range(i, p.nb):
            h, pos = divmod(index, p.half)
            block = agbuf[h, pos * 128 : pos * 128 + 128, :]
            wide = block.astype(F32)
            if i == j:
                wide = wide + eye
                block = wide.astype(BF16)
                square = square + wide * wide
            else:
                square = square + 2.0 * (wide * wide)
                gram[j * 128 : j * 128 + 128, i * 128 : i * 128 + 128] = wide.T.astype(BF16)
            gram[i * 128 : i * 128 + 128, j * 128 : j * 128 + 128] = block
            index += 1
    square = jnp.sum(jnp.sum(square, axis=0, keepdims=True), axis=1, keepdims=True)
    frob = jnp.sqrt(square)
    inv = 1.0 / frob

    strips = p.m // p.strip

    def mm(a, b):
        return jnp.dot(a, b, preferred_element_type=F32)

    def put(ref, s, value):
        cols = slice(s * p.strip, (s + 1) * p.strip)
        value = value.astype(ref.dtype)
        ref[: (s + 1) * p.strip, cols] = value
        if s > 0:
            ref[cols, : s * p.strip] = value[: s * p.strip].T

    def corner(s):
        return slice(0, (s + 1) * p.strip), slice(s * p.strip, (s + 1) * p.strip)

    for s in reversed(range(strips)):
        rows, cols = corner(s)
        unit = gram[rows, cols].astype(F32) * inv
        unit2 = mm(gram[rows, :], gram[:, cols]) * (inv * inv)
        put(prod, s, unit2)
        put(mix, s, 0.0625 * unit2 - 0.5625 * unit)
        est[rows, cols] = 1.6875 * unit2 - 2.4375 * unit
    for s in reversed(range(strips)):
        rows, cols = corner(s)
        new = est[rows, cols] + mm(prod[rows, :], mix[:, cols])
        est[rows, cols] = new
        put(estb, s, new)
    for s in reversed(range(strips)):
        rows, cols = corner(s)
        half = gram[rows, cols].astype(F32) * (2.25 * inv) + mm(gram[rows, :], estb[:, cols]) * inv
        more[rows, cols] = half
        put(prod, s, half)
    for s in reversed(range(strips)):
        rows, cols = corner(s)
        unit = 2.25 * more[rows, cols] + mm(prod[rows, :], estb[:, cols])
        more[rows, cols] = unit
        put(mix, s, unit)
    for s in reversed(range(strips)):
        rows, cols = corner(s)
        unit = more[rows, cols]
        unit2 = mm(mix[rows, :], mix[:, cols])
        put(prod, s, unit2)
        put(moreb, s, 0.0625 * unit2 - 0.5625 * unit)
        more[rows, cols] = 1.6875 * unit2 - 2.4375 * unit
    for s in reversed(range(strips)):
        rows, cols = corner(s)
        new = more[rows, cols] + mm(prod[rows, :], moreb[:, cols])
        put(mix, s, new)
        est[rows, cols] = 2.25 * (est[rows, cols] + new)
    for s in reversed(range(strips)):
        rows, cols = corner(s)
        new = est[rows, cols] + mm(estb[rows, :], mix[:, cols])
        row_ids = lax.broadcasted_iota(jnp.int32, new.shape, 0)
        col_ids = lax.broadcasted_iota(jnp.int32, new.shape, 1) + s * p.strip
        put(est, s, new + jnp.where(row_ids == col_ids, 2.25 * 2.25, 0.0))

    inv_root = lax.rsqrt(frob)

    def shift_rows(s, total):
        rows = pl.ds(pl.multiple_of(s * 128, 128), 128)
        block = est[rows, :]
        midway = jnp.sum(block * prow[...], axis=1, keepdims=True)
        return total + jnp.sum(block * midway, axis=0, keepdims=True)

    shift = lax.fori_loop(0, p.m // 128, shift_rows, jnp.zeros((1, p.m), F32))
    shift = shift * (inv / root_scale)

    def chip_rows(dy):
        return pl.ds(pl.multiple_of(lax.rem(y + dy, p.ny) * 256, 256), 256)

    def transform(dy):
        tmat[chip_rows(dy), :] = (est[chip_rows(dy), :] * inv_root + shift).astype(BF16)

    per_half = p.share // 2

    def out_copy(dy, core, h):
        there = lax.rem(y + dy, p.ny) * 2 + core
        cols = pl.ds(h * per_half, per_half)
        return copy_to(
            stage.at[dy, pl.ds(core * 128, 128), cols], out.at[:, half_cols(n, h)], out_s.at[dy, core, h], out_r.at[n, h], (w, there)
        )

    def out_arrival(k, h):
        cols = pl.ds(h * per_half, per_half)
        slot = out.at[:, half_cols(near(k), h)]
        return copy_to(stage.at[0, pl.ds(0, 128), cols], slot, out_s.at[0, 0, h], out_r.at[near(k), h], (w, near(k)))

    def analyse(dy, h, mean):
        rows = chip_rows(dy)
        if h == 0:
            transform(dy)
        cols = slice(h * per_half, (h + 1) * per_half)
        stage[dy, :, cols] = (mean + mm(tmat[rows, :], anom[:, cols])).astype(BF16)

    order = sorted(range(1, p.ny), key=lambda d: -min(d, p.ny - d))
    means = []
    early, pending = pending, []
    for h in range(2):
        for k in p.near:
            raw_arrival(k, h).wait_recv()
        if h == 0:
            own.wait()
        cols = slice(h * per_half, (h + 1) * per_half)
        mean = jnp.zeros((1, per_half), F32)
        for k in range(p.narrow):
            mean = mean + jnp.sum(raw[k, :, cols].astype(F32), axis=0, keepdims=True)
        mean = mean / p.m
        means.append(mean)
        first = n * (p.share // 128) + h * (per_half // 128)
        factors = [jnp.full((1, 128), infl[owner[first + b]], F32) for b in range(per_half // 128)]
        factors = jnp.concatenate(factors, axis=1)
        for k in range(p.narrow):
            anom[k * 128 : k * 128 + 128, cols] = (factors * (raw[k, :, cols].astype(F32) - mean)).astype(BF16)
        for dy in order:
            analyse(dy, h, mean)
            for core in range(2):
                out_copy(dy, core, h).start()
                pending.append(out_copy(dy, core, h))
    for h in range(2):
        analyse(0, h, means[h])
    rest = []
    for h in range(2):
        cols = pl.ds(h * per_half, per_half)
        theirs = stage.at[0, pl.ds(pl.multiple_of((1 - c) * 128, 128), 128), cols]
        mine = stage.at[0, pl.ds(pl.multiple_of(c * 128, 128), 128), cols]
        to_sibling = copy_to(theirs, out.at[:, half_cols(n, h)], out_s.at[0, 0, h], out_r.at[n, h], sibling)
        to_sibling.start()
        pending.append(to_sibling)
        keep = pltpu.make_async_copy(mine, out.at[:, half_cols(n, h)], own_sem.at[h])
        keep.start()
        rest.append(keep)
    finish(early)
    for keep in rest:
        keep.wait()
    for h in range(2):
        for k in reversed(p.near):
            out_arrival(k, h).wait_recv()
    finish(pending)


def hand_on(parts, done, out, hold, in_sems, out_sems):
    rows = [pl.ds(k * (done.shape[0] // parts), done.shape[0] // parts) for k in range(parts)]
    reads = [pltpu.make_async_copy(done.at[r], hold.at[r], in_sems.at[k]) for k, r in enumerate(rows)]
    writes = [pltpu.make_async_copy(hold.at[r], out.at[r], out_sems.at[k]) for k, r in enumerate(rows)]
    for read in reads:
        read.start()
    for read, write in zip(reads, writes):
        read.wait()
        write.start()
    for write in writes:
        write.wait()


def on_device(grid, narrow, ensemble, owner, inflation, obs_block, obs_value, obs_std):
    p = Plan(grid, narrow, *ensemble.shape, obs_value.shape[0])
    dma = pltpu.SemaphoreType.DMA
    vmem, smem = pl.BlockSpec(memory_space=pltpu.VMEM), pl.BlockSpec(memory_space=pltpu.SMEM)
    anywhere = pl.BlockSpec(memory_space=pl.ANY)
    square = (p.m, p.m)
    scratch = [
        pltpu.VMEM((p.states // 128, p.ml, 128), BF16),
        pltpu.VMEM((p.narrow, p.ml, p.oshare), BF16),
        pltpu.VMEM((p.narrow, p.ml, p.oshare), BF16),
        pltpu.VMEM((p.m, p.oshare), BF16),
        pltpu.VMEM((2, p.peers, p.ra, 128), BF16),
        pltpu.VMEM((2, p.nz, p.tb, 128), BF16),
        pltpu.VMEM((p.peers, p.ra, 128), BF16),
        pltpu.VMEM((p.nz, p.tb, 128), BF16),
        pltpu.VMEM((p.peers, p.ra, 128), BF16),
        pltpu.VMEM((p.nz, p.tb, 128), BF16),
        pltpu.VMEM((p.peers, p.ra, 128), BF16),
        pltpu.VMEM((p.nz, p.tb, 128), BF16),
        pltpu.VMEM((p.nz, p.ra, 128), BF16),
        pltpu.VMEM((p.nx, p.tb, 128), BF16),
        pltpu.VMEM((p.ny, p.tb, 128), BF16),
        pltpu.VMEM((16, 128), F32),
        pltpu.VMEM((1, p.m), F32),
        pltpu.VMEM((2, p.half * 128, 128), BF16),
        pltpu.VMEM(square, BF16),
        pltpu.VMEM(square, BF16),
        pltpu.VMEM(square, BF16),
        pltpu.VMEM(square, F32),
        pltpu.VMEM(square, BF16),
        pltpu.VMEM(square, F32),
        pltpu.VMEM(square, BF16),
        pltpu.VMEM((p.narrow, p.ml, p.share), BF16),
        pltpu.VMEM((p.m, p.share), BF16),
        pltpu.VMEM(square, BF16),
        pltpu.VMEM((p.ny, 256, p.share), BF16),
        dma, dma((p.narrow,)), dma((p.narrow,)),
        dma((2,)), dma((2,)),
        dma((p.peers,)), dma((p.peers,)), dma((p.nz,)), dma((p.nz,)),
        dma((p.nz,)), dma((p.nz,)), dma((p.nx,)), dma((p.nx,)), dma((p.ny,)), dma((p.ny,)),
        dma((p.peers,)), dma((p.peers,)), dma((p.nz,)), dma((p.nz,)),
        dma((p.peers,)), dma((p.peers,)), dma((p.nz,)), dma((p.nz,)),
        dma((p.narrow, 2)), dma((p.narrow, 2)),
        dma((2,)), dma((p.ny, 2, 2)), dma((p.narrow, 2)),
    ]
    done = pl.pallas_call(
        functools.partial(kernel, p),
        out_shape=jax.ShapeDtypeStruct(ensemble.shape, BF16),
        in_specs=[smem, smem, smem, anywhere, vmem, vmem],
        out_specs=anywhere,
        scratch_shapes=scratch,
        compiler_params=pltpu.CompilerParams(
            collective_id=0, has_side_effects=True, vmem_limit_bytes=56 * 1024 * 1024
        ),
        name="etkf",
    )(owner, inflation, obs_block, ensemble, obs_value.reshape(-1, 128), obs_std.reshape(-1, 128))
    parts = p.ml // 16
    return pl.pallas_call(
        functools.partial(hand_on, parts),
        out_shape=jax.ShapeDtypeStruct(ensemble.shape, BF16),
        in_specs=[anywhere],
        out_specs=anywhere,
        scratch_shapes=[pltpu.VMEM(ensemble.shape, BF16), dma((parts,)), dma((parts,))],
        compiler_params=pltpu.CompilerParams(vmem_limit_bytes=56 * 1024 * 1024),
        name="hand_on",
    )(done)


def solution(mesh):
    wide, narrow = mesh.shape["wide"], mesh.shape["narrow"]
    grid = (4, wide // 4) if wide >= 16 else (2, wide // 2)
    return jax.shard_map(
        functools.partial(on_device, grid, narrow),
        mesh=mesh,
        in_specs=(P("narrow", "wide"), P("wide"), P(), P("wide"), P("wide"), P("wide")),
        out_specs=P("narrow", "wide"),
        check_vma=False,
    )
```
